512 devices in a mesh: dp: 32 (over z_hi, x, y), seq: 16 (over z_lo, core).
Axes of the slice: x: 4, y: 4, z: 16 (z_hi: 2, z_lo: 8; z = z_hi * 8 + z_lo), core: 2. Of those that a mesh axis runs over, the one named last changes fastest.
Arguments:
- tokens: bfloat16 [32, 2048, 1024], P('dp', 'seq'), may hold values from -12 to 12, as said below
- grad_out: bfloat16 [32, 2048, 1024], P('dp', 'seq'), may hold values from -6 to 6
- stacked: bfloat16 [1024, 4, 512], P('seq'), may hold values from -0.176776695 to 0.176776695, as said below
Outputs:
- layer_out: bfloat16 [32, 2048, 1024], P('dp', 'seq')
- grad_tokens: bfloat16 [32, 2048, 1024], P('dp', 'seq')
- grad_weights: float32 [1024, 4, 512], P('seq')
The draws below stay inside these ranges and needn't reach their ends.
Inputs may be any that keep to these rules, and one draw needn't show every extreme that they name: `tokens`: activations of order one. `stacked`: entries scaled by the inverse square root of their fan-in.
All inputs are finite; a program needn't handle non-finite values.
Results may differ from the reference program's by a relative error of at most 0.035.
Values may be sent and summed in bfloat16 or wider, within the bound.
No kernel may reach another device: no remote copies, remote signals or barrier semaphores. Data moves between devices by JAX's collectives and lax.ppermute only.
A program may use at most 64 MiB of HBM per device.

```python
import math
import jax
import jax.numpy as jnp
from jax import lax

D = 1024
HEADS = 8
HEAD = 64
LEAF = 128
SEQS = 1
HD = 512
BATCH = 32
LEN = 2048
N_DP = 32
N_SEQ = 16


def draw_tokens(key, part):
    key = jax.random.fold_in(key, 11)
    base_key = jax.random.fold_in(key, 0)
    shape = (BATCH, LEN, D)
    return jnp.clip(jax.random.normal(base_key, shape, jnp.float32), -4.0, 4.0).astype(jnp.bfloat16)


def draw_stacked(key, part):
    key = jax.random.fold_in(key, 23)
    shape = (D, 4, HD)
    slot_ids = jnp.arange(4).reshape(1, 4, 1)
    fan_scale = jnp.where(slot_ids < 3, 1.0 / math.sqrt(D), 1.0 / math.sqrt(HD))
    raw = jnp.clip(jax.random.normal(key, shape, jnp.float32), -4.0, 4.0)
    return (raw * fan_scale).astype(jnp.bfloat16)


def strengthened(array, own_key, source, target, shards_of, factor):
    owner, partner = [(jnp.arange(array.shape[dim]) // (array.shape[dim] // shards_of)).reshape([-1 if axis == dim else 1 for axis in range(array.ndim)]) for dim in (source, target)]
    chosen = jax.random.permutation(own_key, shards_of)[partner]
    strong = (owner == chosen) | (owner == (partner + shards_of // 2) % shards_of)
    return jnp.where(strong, factor * array, array)


def block_scale(stream_key, shape, pieces, least, top_value):
    factor_of = 1.0
    for position, parts in pieces:
        heights = jax.random.uniform(jax.random.fold_in(jax.random.fold_in(stream_key, 6), position), (parts,), jnp.float32, least / len(pieces), top_value / len(pieces))
        factor_of = factor_of * jnp.repeat(jnp.exp(heights), shape[position] // parts).reshape((-1,) + (1,) * (len(shape) - 1 - position))
    return factor_of


def bell_draw_with(rng, extent, scale, limit, pieces, heavy, held_as=jnp.bfloat16):
    entries = scale * jax.random.normal(rng, extent, jnp.float32)
    if pieces:
        entries = entries * block_scale(rng, extent, pieces, -0.22, 0.18)
    return jnp.clip(strengthened(entries, jax.random.fold_in(rng, 3), *heavy), -limit, limit).astype(held_as)


def setup_inputs(seed: int = 0) -> dict:
    keys = jax.random.split(jax.random.key(seed), 4)
    tokens = draw_tokens(jax.random.fold_in(keys[3], 71), 0)
    grad_out = bell_draw_with(keys[1], (BATCH, LEN, D), 1.0, 6.0, ((0, 32), (1, 16)), (1, 2, 16, 2.0))
    stacked = draw_stacked(jax.random.fold_in(keys[3], 71), 0)
    return {"tokens": tokens, "grad_out": grad_out, "stacked": stacked}


LOG_TWO = math.log(2.0)

def pair_mean(blocks):
    widened = blocks.astype(jnp.float32)
    paired = widened.reshape(widened.shape[:-2] + (widened.shape[-2] // 2, 2, widened.shape[-1]))
    return (0.5 * (paired[..., 0, :] + paired[..., 1, :])).astype(jnp.bfloat16)

def swap_blocks(blocks, height):
    stride = 2 ** height
    tally = blocks.shape[1]
    shaped = blocks.reshape((blocks.shape[0], tally // (2 * stride), 2, stride) + blocks.shape[2:])
    return jnp.flip(shaped, 2).reshape(blocks.shape)

def sequence_pass(seq_tokens, seq_grads, stacked):
    blocks = N_SEQ
    levels = blocks.bit_length() - 1
    width = stacked.shape[2]
    qkv_weight = stacked[:, :3, :].reshape(D, 3 * width)
    out_weight = stacked[:, 3, :]
    projected = jnp.dot(seq_tokens, qkv_weight, preferred_element_type=jnp.float32).astype(jnp.bfloat16)
    queries = projected[:, :width].reshape(blocks, LEAF, width)
    key_value = jnp.stack([projected[:, width:2 * width], projected[:, 2 * width:]])
    leaves = key_value.reshape(2, blocks, LEAF, width)
    grad_attn = jnp.dot(seq_grads, out_weight, preferred_element_type=jnp.float32).astype(jnp.bfloat16)
    siblings = []
    current = key_value
    for height in range(levels):
        coarse = current.reshape(2, blocks >> height, LEAF, width)
        swapped = swap_blocks(coarse, 0)
        siblings.append(jnp.repeat(swapped, 2 ** height, axis=1))
        current = pair_mean(current)
    key_sets = jnp.concatenate([leaves] + siblings, axis=2)
    key_count = key_sets.shape[2]
    offsets = jnp.maximum(jnp.arange(key_count) // LEAF - 1, 0).astype(jnp.float32) * LOG_TWO
    score_scale = 1.0 / math.sqrt(HEAD)
    query_wide = queries.reshape(blocks, LEAF, HEADS, HEAD).astype(jnp.float32)
    key_wide = key_sets[0].reshape(blocks, key_count, HEADS, HEAD).astype(jnp.float32)
    value_wide = key_sets[1].reshape(blocks, key_count, HEADS, HEAD).astype(jnp.float32)
    grad_wide = grad_attn.reshape(blocks, LEAF, HEADS, HEAD).astype(jnp.float32)
    scores = jnp.einsum('nqhe,nkhe->nhqk', query_wide, key_wide) * score_scale + offsets
    row_peak = lax.optimization_barrier(jnp.max(scores, axis=-1, keepdims=True))
    exponent = jnp.exp(scores - row_peak)
    weights = exponent / lax.optimization_barrier(jnp.sum(exponent, axis=-1, keepdims=True))
    weights_low = weights.astype(jnp.bfloat16).astype(jnp.float32)
    attended = jnp.einsum('nhqk,nkhe->nqhe', weights_low, value_wide).astype(jnp.bfloat16)
    attended = attended.reshape(LEN, width)
    layer = jnp.dot(attended, out_weight.T, preferred_element_type=jnp.float32).astype(jnp.bfloat16)
    dprobs = jnp.einsum('nqhe,nkhe->nhqk', grad_wide, value_wide)
    rowdot = lax.optimization_barrier(jnp.sum(weights * dprobs, axis=-1, keepdims=True))
    dscore = (weights * (dprobs - rowdot) * score_scale).astype(jnp.bfloat16).astype(jnp.float32)
    dquery = jnp.einsum('nhqk,nkhe->nqhe', dscore, key_wide).astype(jnp.bfloat16).reshape(LEN, width)
    key_grad = jnp.einsum('nhqk,nqhe->nkhe', dscore, query_wide).reshape(blocks, key_count, width)
    value_grad = jnp.einsum('nhqk,nqhe->nkhe', weights_low, grad_wide).reshape(blocks, key_count, width)
    grads = jnp.stack([key_grad, value_grad])
    held = None
    for height in reversed(range(levels)):
        piece = grads[:, :, (height + 1) * LEAF:(height + 2) * LEAF]
        rounded = lax.optimization_barrier(piece.astype(jnp.bfloat16)).astype(jnp.float32)
        grouped = lax.optimization_barrier(jnp.sum(rounded.reshape(2, blocks >> height, 2 ** height, LEAF, width), axis=2))
        level_sum = swap_blocks(grouped, 0).reshape(2, (blocks >> height) * LEAF, width)
        if held is not None:
            level_sum = level_sum + jnp.repeat(0.5 * held, 2, axis=1)
        held = level_sum
    own_grads = (grads[:, :, :LEAF] + held.reshape(2, blocks, LEAF, width)).astype(jnp.bfloat16)
    back_all = jnp.concatenate([dquery, own_grads[0].reshape(LEN, width), own_grads[1].reshape(LEN, width)], axis=-1)
    back = jnp.dot(back_all, qkv_weight.T, preferred_element_type=jnp.float32).astype(jnp.bfloat16)
    left_tokens = seq_tokens.reshape(blocks, LEAF, D).astype(jnp.float32)
    left_grads = seq_grads.reshape(blocks, LEAF, D).astype(jnp.float32)
    term_inputs = jnp.einsum('nld,nlf->ndf', left_tokens, back_all.reshape(blocks, LEAF, 3 * width).astype(jnp.float32))
    term_output = jnp.einsum('nld,nlf->ndf', left_grads, attended.reshape(blocks, LEAF, width).astype(jnp.float32))
    return (layer, back, jnp.concatenate([term_inputs, term_output], axis=-1))

def reference(tokens, grad_out, stacked):
    grouped_tokens = tokens.reshape(N_DP, SEQS, LEN, D)
    grouped_grads = grad_out.reshape(N_DP, SEQS, LEN, D)

    def group_step(accumulated, group_data):
        group_tokens, group_grads = group_data
        layers = []
        backs = []
        block_sum = jnp.zeros((N_SEQ, D, 4 * HD), jnp.float32)
        for member in range(SEQS):
            layer, back, term = sequence_pass(group_tokens[member], group_grads[member], stacked)
            layers.append(layer)
            backs.append(back)
            block_sum = block_sum + term
        rounded = lax.optimization_barrier(block_sum.astype(jnp.bfloat16))
        accumulated = accumulated + lax.optimization_barrier(jnp.sum(rounded.astype(jnp.float32), axis=0))
        return (accumulated, (jnp.stack(layers), jnp.stack(backs)))
    start_sum = jnp.zeros((D, 4 * HD), jnp.float32)
    final_sum, outputs = lax.scan(group_step, start_sum, (grouped_tokens, grouped_grads))
    grad_weights = (final_sum * (1.0 / math.sqrt(BATCH * LEN))).reshape(D, 4, HD)
    return (outputs[0].reshape(BATCH, LEN, D), outputs[1].reshape(BATCH, LEN, D), grad_weights)
```

```python
import functools
import math

import jax
import jax.numpy as jnp
import numpy as np
from jax import lax
from jax.experimental import pallas as pl
from jax.experimental.pallas import tpu as pltpu
from jax.sharding import PartitionSpec as P

HEAD = 64
LOG_TWO = math.log(2.0)
BF = jnp.bfloat16
F32 = jnp.float32

ROW_LEVELS = ((0, 256, 0), (256, 320, 2), (320, 384, 3), (384, 512, 1), (512, 576, 2), (576, 640, 3))


def nn(a, b):
    return lax.dot_general(a, b, (((1,), (0,)), ((), ())), preferred_element_type=F32)


def nt(a, b):
    return lax.dot_general(a, b, (((1,), (1,)), ((), ())), preferred_element_type=F32)


def layer_kernel(nx, ny, pos_ref, tok_ref, tokt_ref, g_ref, gt_ref, w0, p1, p2, p3, p4, m1, m2, m3, m4,
                 w_ref, part_ref, lown_ref, lsend_ref, dq_ref, gown_ref, gkeep_ref, gsend_ref,
                 kv_s, kvt_s, qm_s, gm_s, gkv_s, attt_s, dqt_s, att_s):
    zl = pos_ref[0]
    core = pos_ref[1]

    def place(index, piece):
        row = pl.multiple_of(lax.rem(zl + index + 8, 8) * 128, 128)
        w_ref[pl.ds(row, 128), :] = piece

    place(0, w0[...])
    for index, piece in ((1, p1), (2, p2), (3, p3), (-1, m1), (-2, m2), (-3, m3)):
        place(index, piece[...])
    place(4, jnp.concatenate([p4[...], m4[...]], axis=0))

    def project_keys(step, carry):
        row = pl.multiple_of(step * 128, 128)
        block = nn(tok_ref[pl.ds(row, 128), :], w_ref[:, 256:768])
        kv_s[pl.ds(row, 128), :] = block.astype(BF)
        kvt_s[:, pl.ds(row, 128)] = block.T.astype(BF)
        return carry

    lax.fori_loop(0, 5, project_keys, 0)
    queries = nn(tok_ref[0:256, :], w_ref[:, 0:256]) * 0.125
    grads = nn(g_ref[...], w_ref[:, 768:1024])
    lane = lax.broadcasted_iota(jnp.int32, (256, 128), 1)
    for head in range(4):
        pair = (head // 2) * 128
        mine = (lane >= 64) if head % 2 else (lane < 64)
        qm_s[head] = jnp.where(mine, queries[:, pair:pair + 128], 0.0).astype(BF)
        gm_s[head] = jnp.where(mine, grads[:, pair:pair + 128], 0.0).astype(BF)

    for pair in range(2):
        kcol = pair * 128
        vcol = 256 + pair * 128
        key_grad = None
        value_grad = None
        for half in range(2):
            head = 2 * pair + half
            qm = qm_s[head]
            gm = gm_s[head]
            raw = nt(kv_s[:, kcol:kcol + 128], qm)
            scores = jnp.concatenate(
                [raw[lo:hi] + level * LOG_TWO if level else raw[lo:hi] for lo, hi, level in ROW_LEVELS], axis=0)
            exponent = jnp.exp(scores - jnp.max(scores, axis=0, keepdims=True))
            weights = exponent * (1.0 / jnp.sum(exponent, axis=0, keepdims=True))
            low = weights.astype(BF)
            dprobs = nt(kv_s[:, vcol:vcol + 128], gm)
            rowdot = jnp.sum(weights * dprobs, axis=0, keepdims=True)
            dscore = (weights * (dprobs - rowdot)).astype(BF)
            rows = slice(head * 64, head * 64 + 64)
            attt_s[rows, :] = nn(kvt_s[256 + head * 64:320 + head * 64, :], low)
            dqt_s[rows, :] = nn(kvt_s[rows, :], dscore) * 0.125
            new_key = nn(dscore, qm)
            new_value = nn(low, gm)
            key_grad = new_key if key_grad is None else key_grad + new_key
            value_grad = new_value if value_grad is None else value_grad + new_value
        for col, grad in ((kcol, key_grad), (vcol, value_grad)):
            cols = slice(col, col + 128)
            gown_ref[:, cols] = grad[0:256]
            gkeep_ref[:, cols] = grad[256:384]
            gkv_s[:, cols] = grad.astype(BF)

    gsend_ref[...] = gkv_s[384:640, :]
    dq_ref[...] = dqt_s[...].T.astype(BF)
    attended = attt_s[...].T.astype(BF)
    att_s[0] = attended[0:128]
    att_s[1] = attended[128:256]

    x_rows = 64 // nx
    y_cols = 1024 // ny

    def grad_rows(step, carry):
        rows = pl.ds(pl.multiple_of(step * 128, 128), 128)
        lhs = tokt_ref[rows, :]
        att_all = jnp.concatenate([att_s[0], att_s[1]], axis=0)
        block = jnp.concatenate(
            [nn(lhs[:, 0:256], dq_ref[...]).astype(BF), nn(lhs, gkv_s[...]).astype(BF),
             nn(gt_ref[rows, :], att_all).astype(BF)], axis=1)
        for side in range(2):
            for x in range(nx):
                for y in range(ny):
                    part_ref[x * ny + y, 2 * step + side] = block[
                        side * 64 + x * x_rows:side * 64 + (x + 1) * x_rows, y * y_cols:(y + 1) * y_cols]
        return carry

    lax.fori_loop(0, 8, grad_rows, 0)
    lown_ref[...] = nt(att_s[core], w_ref[:, 768:1024])
    lsend_ref[...] = nt(att_s[1 - core], w_ref[:, 768:1024]).astype(BF)


def run_layer(nx, ny, *operands):
    vmem = pl.BlockSpec(memory_space=pltpu.VMEM)
    smem = pl.BlockSpec(memory_space=pltpu.SMEM)
    shape = jax.ShapeDtypeStruct
    return pl.pallas_call(
        functools.partial(layer_kernel, nx, ny),
        out_shape=(
            shape((1024, 1024), BF),
            shape((nx * ny, 16, 64 // nx, 1024 // ny), BF),
            shape((128, 1024), F32),
            shape((128, 1024), BF),
            shape((256, 256), BF),
            shape((256, 512), F32),
            shape((128, 512), F32),
            shape((256, 512), BF),
        ),
        in_specs=[smem] + [vmem] * (len(operands) - 1),
        out_specs=tuple([vmem] * 8),
        scratch_shapes=[
            pltpu.VMEM((640, 512), BF),
            pltpu.VMEM((512, 640), BF),
            pltpu.VMEM((4, 256, 128), BF),
            pltpu.VMEM((4, 256, 128), BF),
            pltpu.VMEM((640, 512), BF),
            pltpu.VMEM((256, 256), F32),
            pltpu.VMEM((256, 256), F32),
            pltpu.VMEM((2, 128, 256), BF),
        ],
        compiler_params=pltpu.CompilerParams(vmem_limit_bytes=40 * 1024 * 1024),
        cost_estimate=pl.CostEstimate(flops=3_500_000_000, bytes_accessed=14_000_000, transcendentals=700_000),
    )(*operands)


def coarsening():
    matrix = np.zeros((224, 256), np.float32)
    base = 0
    for level in (1, 2, 3):
        for row in range(256 >> level):
            matrix[base + row, row << level:(row + 1) << level] = 0.5 ** level
        base += 256 >> level
    return matrix


def make_device(nx, ny, dp_count, seq_count):
    nxy = nx * ny
    nzh = dp_count // nxy
    ring = nzh * 8
    core_pairs = [(i, i ^ 1) for i in range(seq_count)]

    def chip_swap(bit):
        return [(i, i ^ (2 << bit)) for i in range(seq_count)]

    def along_z(shift):
        pairs = []
        for z in range(ring):
            source = (z + shift) % ring
            for xy in range(nxy):
                for core in range(2):
                    pairs.append((((source // 8) * nxy + xy) * seq_count + (source % 8) * 2 + core,
                                  ((z // 8) * nxy + xy) * seq_count + (z % 8) * 2 + core))
        return pairs

    plus, minus = along_z(1), along_z(-1)
    plane_groups = [[zh * nxy + xy for xy in range(nxy)] for zh in range(nzh)]
    zh_pairs = [(zh * nxy + xy, ((zh + 1) % nzh) * nxy + xy) for zh in range(nzh) for xy in range(nxy)]
    coarse_matrix = coarsening()

    def swap_core(value):
        return lax.ppermute(value, "seq", core_pairs)

    def per_device(tokens, grad_out, stacked):
        seq = lax.axis_index("seq")
        zl = seq >> 1
        core = seq & 1
        first = core == 0

        def ordered(mine, other, axis):
            return jnp.where(first, jnp.concatenate([mine, other], axis), jnp.concatenate([other, mine], axis))

        shard = stacked.reshape(64, 4, 2, 256)
        keep = lax.dynamic_index_in_dim(shard, core, 2, False).reshape(64, 1024)
        give = lax.dynamic_index_in_dim(shard, 1 - core, 2, False).reshape(64, 1024)
        w0 = ordered(keep, swap_core(give), 0)
        both = ("dp", "seq")
        p1 = lax.ppermute(w0, both, plus)
        m1 = lax.ppermute(w0, both, minus)
        p2 = lax.ppermute(p1, both, plus)
        m2 = lax.ppermute(m1, both, minus)
        p3 = lax.ppermute(p2, both, plus)
        m3 = lax.ppermute(m2, both, minus)
        p4 = lax.ppermute(p3[0:64], both, plus)
        m4 = lax.ppermute(m3[64:128], both, minus)

        own = jnp.concatenate([tokens[0], grad_out[0]], axis=0)
        got = swap_core(own)
        chip_tokens = ordered(own[0:128], got[0:128], 0)
        chip_grads = ordered(own[128:256], got[128:256], 0)
        matrix = jnp.asarray(coarse_matrix, BF)
        half_tokens = lax.dynamic_slice(chip_tokens, (0, core * 512), (256, 512))
        coarse = nn(matrix, half_tokens).astype(BF)
        c1, c2, c3 = coarse[0:128], coarse[128:192], coarse[192:224]
        r3 = lax.ppermute(c3, "seq", chip_swap(2))
        second = lax.ppermute(jnp.concatenate([c2, r3], 0), "seq", chip_swap(1))
        held = jnp.concatenate([second[0:64], r3, second[64:96]], 0)
        third = lax.ppermute(jnp.concatenate([c1, held], 0), "seq", chip_swap(0))
        half_set = jnp.concatenate([held, third], 0)
        rest = ordered(half_set, swap_core(half_set), 1)
        token_set = jnp.concatenate([chip_tokens, rest], 0)

        position = jnp.stack([zl, core]).astype(jnp.int32)
        (weight, part, layer_own, layer_send, dquery, grad_own, grad_keep, grad_send) = run_layer(
            nx, ny, position, token_set, token_set.T, chip_grads, chip_grads.T,
            w0, p1, p2, p3, p4, m1, m2, m3, m4)

        if nxy > 1:
            pieces = lax.all_to_all(part, "dp", 0, 0, axis_index_groups=plane_groups, tiled=True)
        else:
            pieces = part
        plane_sum = jnp.sum(pieces.astype(F32), axis=0).astype(BF)
        columns = lax.all_to_all(plane_sum, "seq", 0, 0, tiled=True)
        rows, cols = 64 // nx, 1024 // ny
        line_sum = jnp.sum(columns.astype(F32).reshape(8, 2, rows, cols), axis=0).astype(BF)
        if nzh > 1:
            other_half = lax.ppermute(line_sum, "dp", zh_pairs)
            line_sum = (line_sum.astype(F32) + other_half.astype(F32)).astype(BF)
        spread = jnp.broadcast_to(line_sum[None], (nxy, 2, rows, cols))
        if nxy > 1:
            spread = lax.all_to_all(spread, "dp", 0, 0, axis_index_groups=plane_groups, tiled=True)
        slots = 4 // ny
        full = spread.reshape(nx, ny, 2, rows, slots, 256).transpose(0, 3, 1, 4, 2, 5).reshape(64, 4, 512)
        total = 128 * seq_count * dp_count
        grad_weights = full.astype(F32) * (1.0 / math.sqrt(total))

        layer_out = (layer_own + swap_core(layer_send).astype(F32)).astype(BF)

        b1 = lax.ppermute(grad_send, "seq", chip_swap(0))
        joined = grad_keep + b1[128:256].astype(F32)
        b2 = lax.ppermute(jnp.concatenate([joined[0:64], joined[96:128]], 0).astype(BF), "seq", chip_swap(1))
        b3 = lax.ppermute((joined[64:96] + b2[64:96].astype(F32)).astype(BF), "seq", chip_swap(2))
        returned = jnp.concatenate([b1[0:128], b2[0:64], b3], 0)
        dkv = (grad_own + nn(jnp.asarray(coarse_matrix.T, BF), returned)).astype(BF)
        back = jnp.concatenate([dquery, dkv], axis=1)
        partial = nt(back, weight[:, 0:768])
        mine = lax.dynamic_slice(partial, (core * 128, 0), (128, 1024))
        theirs = lax.dynamic_slice(partial, ((1 - core) * 128, 0), (128, 1024)).astype(BF)
        grad_tokens = (mine + swap_core(theirs).astype(F32)).astype(BF)
        return layer_out[None], grad_tokens[None], grad_weights

    return per_device


def solution(mesh):
    dp_count, seq_count = mesh.shape["dp"], mesh.shape["seq"]
    side = 4 if dp_count >= 16 else (2 if dp_count >= 4 else 1)
    specs = (P("dp", "seq", None), P("dp", "seq", None), P("seq", None, None))
    return jax.shard_map(
        make_device(side, side, dp_count, seq_count),
        mesh=mesh, in_specs=specs, out_specs=specs, check_vma=False)
```

```python
import functools
import math

import jax
import jax.numpy as jnp
import numpy as np
from jax import lax
from jax.experimental import pallas as pl
from jax.experimental.pallas import tpu as pltpu
from jax.sharding import PartitionSpec as P

HEAD = 64
LOG_TWO = math.log(2.0)
BF = jnp.bfloat16
F32 = jnp.float32

ROW_LEVELS = ((0, 256, 0), (256, 320, 2), (320, 384, 3), (384, 512, 1), (512, 576, 2), (576, 640, 3))


def nn(a, b):
    return lax.dot_general(a, b, (((1,), (0,)), ((), ())), preferred_element_type=F32)


def nt(a, b):
    return lax.dot_general(a, b, (((1,), (1,)), ((), ())), preferred_element_type=F32)


def layer_kernel(nx, ny, pos_ref, *refs):
    sources, refs = refs[:11], refs[11:]
    results, refs = refs[:8], refs[8:]
    staged, refs = refs[:8], refs[8:]
    (tok_s, tokt_s, g_s, gt_s, kv_s, kvt_s, qm_s, gm_s, gkv_s, attt_s, dqt_s, att_s, in_sem, w_sem, out_sem, part_sem) = refs
    tok, tokt, g, gt, w0, r1, r2, r3, r4, x12, x34 = sources
    w_s, part_s, lown_s, lsend_s, dq_s, gown_s, gkeep_s, gsend_s = staged
    zl = pos_ref[0]
    core = pos_ref[1]
    step_sign = 1 - 2 * core
    cols = pl.ds(pl.multiple_of(core * 1024, 1024), 1024)

    def row_of(index):
        return pl.multiple_of(lax.rem(zl + index + 8, 8) * 128, 128)

    def weight_rows(index):
        return w_s.at[pl.ds(row_of(index), 128), :]

    def opposite(which):
        return w_s.at[pl.ds(pl.multiple_of(row_of(4) + which * 64, 64), 64), :]

    moves = [(w0.at[:, cols], weight_rows(0))]
    for k, piece in ((1, r1), (2, r2), (3, r3)):
        moves.append((piece.at[:, cols], weight_rows(step_sign * k)))
    moves.append((r4.at[:, cols], opposite(core)))
    moves.append((x12.at[pl.ds(0, 128), :], weight_rows(-step_sign)))
    moves.append((x12.at[pl.ds(128, 128), :], weight_rows(-2 * step_sign)))
    moves.append((x34.at[pl.ds(0, 128), :], weight_rows(-3 * step_sign)))
    moves.append((x34.at[pl.ds(128, 64), :], opposite(1 - core)))
    weight_copies = [pltpu.make_async_copy(src, dst, w_sem.at[i]) for i, (src, dst) in enumerate(moves)]
    inputs = [pltpu.make_async_copy(src, dst, in_sem.at[i])
              for i, (src, dst) in enumerate(((tok, tok_s), (g, g_s), (tokt, tokt_s), (gt, gt_s)))]
    for copy in inputs[:1] + weight_copies + inputs[1:]:
        copy.start()
    outputs = {i: pltpu.make_async_copy(staged[i], results[i], out_sem.at[i]) for i in (0, 2, 3, 4, 5, 6, 7)}
    inputs[0].wait()
    for copy in weight_copies:
        copy.wait()
    outputs[0].start()

    def project_keys(step, carry):
        row = pl.multiple_of(step * 128, 128)
        block = nn(tok_s[pl.ds(row, 128), :], w_s[:, 256:768])
        kv_s[pl.ds(row, 128), :] = block.astype(BF)
        kvt_s[:, pl.ds(row, 128)] = block.T.astype(BF)
        return carry

    lax.fori_loop(0, 5, project_keys, 0)
    queries = nn(tok_s[0:256, :], w_s[:, 0:256]) * 0.125
    inputs[1].wait()
    grads = nn(g_s[...], w_s[:, 768:1024])
    lane = lax.broadcasted_iota(jnp.int32, (256, 128), 1)
    for head in range(4):
        pair = (head // 2) * 128
        mine = (lane >= 64) if head % 2 else (lane < 64)
        qm_s[head] = jnp.where(mine, queries[:, pair:pair + 128], 0.0).astype(BF)
        gm_s[head] = jnp.where(mine, grads[:, pair:pair + 128], 0.0).astype(BF)

    for pair in range(2):
        kcol = pair * 128
        vcol = 256 + pair * 128
        key_grad = None
        value_grad = None
        for half in range(2):
            head = 2 * pair + half
            qm = qm_s[head]
            gm = gm_s[head]
            raw = nt(kv_s[:, kcol:kcol + 128], qm)
            scores = jnp.concatenate(
                [raw[lo:hi] + level * LOG_TWO if level else raw[lo:hi] for lo, hi, level in ROW_LEVELS], axis=0)
            exponent = jnp.exp(scores - jnp.max(scores, axis=0, keepdims=True))
            weights = exponent * (1.0 / jnp.sum(exponent, axis=0, keepdims=True))
            low = weights.astype(BF)
            dprobs = nt(kv_s[:, vcol:vcol + 128], gm)
            rowdot = jnp.sum(weights * dprobs, axis=0, keepdims=True)
            dscore = (weights * (dprobs - rowdot)).astype(BF)
            rows = slice(head * 64, head * 64 + 64)
            attt_s[rows, :] = nn(kvt_s[256 + head * 64:320 + head * 64, :], low)
            dqt_s[rows, :] = nn(kvt_s[rows, :], dscore) * 0.125
            new_key = nn(dscore, qm)
            new_value = nn(low, gm)
            key_grad = new_key if key_grad is None else key_grad + new_key
            value_grad = new_value if value_grad is None else value_grad + new_value
        for col, grad in ((kcol, key_grad), (vcol, value_grad)):
            where = slice(col, col + 128)
            gown_s[:, where] = grad[0:256]
            gkeep_s[:, where] = grad[256:384]
            gkv_s[:, where] = grad.astype(BF)

    gsend_s[...] = gkv_s[384:640, :]
    dq_s[...] = dqt_s[...].T.astype(BF)
    attended = attt_s[...].T.astype(BF)
    att_s[0] = attended[0:128]
    att_s[1] = attended[128:256]
    for index in (4, 5, 6, 7):
        outputs[index].start()

    x_rows = 64 // nx
    y_cols = 1024 // ny
    inputs[2].wait()
    inputs[3].wait()

    def part_copy(step):
        where = pl.ds(2 * step, 2)
        return pltpu.make_async_copy(part_s.at[:, where], results[1].at[:, where], part_sem.at[step])

    def grad_rows(step, carry):
        rows = pl.ds(pl.multiple_of(step * 128, 128), 128)
        lhs = tokt_s[rows, :]
        att_all = jnp.concatenate([att_s[0], att_s[1]], axis=0)
        block = jnp.concatenate(
            [nn(lhs[:, 0:256], dq_s[...]).astype(BF), nn(lhs, gkv_s[...]).astype(BF),
             nn(gt_s[rows, :], att_all).astype(BF)], axis=1)
        for side in range(2):
            for x in range(nx):
                for y in range(ny):
                    part_s[x * ny + y, 2 * step + side] = block[
                        side * 64 + x * x_rows:side * 64 + (x + 1) * x_rows, y * y_cols:(y + 1) * y_cols]
        part_copy(step).start()
        return carry

    lax.fori_loop(0, 8, grad_rows, 0)
    lown_s[...] = nt(att_s[core], w_s[:, 768:1024])
    lsend_s[...] = nt(att_s[1 - core], w_s[:, 768:1024]).astype(BF)
    outputs[2].start()
    outputs[3].start()
    for step in range(8):
        part_copy(step).wait()
    for index in (0, 2, 3, 4, 5, 6, 7):
        outputs[index].wait()


def run_layer(nx, ny, *operands):
    anywhere = pl.BlockSpec(memory_space=pl.ANY)
    smem = pl.BlockSpec(memory_space=pltpu.SMEM)
    results = (
        ((1024, 1024), BF),
        ((nx * ny, 16, 64 // nx, 1024 // ny), BF),
        ((128, 1024), F32),
        ((128, 1024), BF),
        ((256, 256), BF),
        ((256, 512), F32),
        ((128, 512), F32),
        ((256, 512), BF),
    )
    return pl.pallas_call(
        functools.partial(layer_kernel, nx, ny),
        out_shape=tuple(jax.ShapeDtypeStruct(*result) for result in results),
        in_specs=[smem] + [anywhere] * (len(operands) - 1),
        out_specs=tuple([anywhere] * len(results)),
        scratch_shapes=[pltpu.VMEM(*result) for result in results] + [
            pltpu.VMEM((640, 1024), BF),
            pltpu.VMEM((1024, 640), BF),
            pltpu.VMEM((256, 1024), BF),
            pltpu.VMEM((1024, 256), BF),
            pltpu.VMEM((640, 512), BF),
            pltpu.VMEM((512, 640), BF),
            pltpu.VMEM((4, 256, 128), BF),
            pltpu.VMEM((4, 256, 128), BF),
            pltpu.VMEM((640, 512), BF),
            pltpu.VMEM((256, 256), F32),
            pltpu.VMEM((256, 256), F32),
            pltpu.VMEM((2, 128, 256), BF),
            pltpu.SemaphoreType.DMA((4,)),
            pltpu.SemaphoreType.DMA((9,)),
            pltpu.SemaphoreType.DMA((8,)),
            pltpu.SemaphoreType.DMA((8,)),
        ],
        compiler_params=pltpu.CompilerParams(vmem_limit_bytes=28 * 1024 * 1024),
        cost_estimate=pl.CostEstimate(flops=3_500_000_000, bytes_accessed=14_000_000, transcendentals=700_000),
    )(*operands)


def coarsening():
    matrix = np.zeros((224, 256), np.float32)
    base = 0
    for level in (1, 2, 3):
        for row in range(256 >> level):
            matrix[base + row, row << level:(row + 1) << level] = 0.5 ** level
        base += 256 >> level
    return matrix


def make_device(nx, ny, dp_count, seq_count):
    nxy = nx * ny
    nzh = dp_count // nxy
    ring = nzh * 8
    core_pairs = [(i, i ^ 1) for i in range(seq_count)]

    def chip_swap(bit):
        return [(i, i ^ (2 << bit)) for i in range(seq_count)]

    def device(z, xy, core):
        return ((z // 8) * nxy + xy) * seq_count + (z % 8) * 2 + core

    ring_pairs = [(device((z + 1 - 2 * core) % ring, xy, core), device(z, xy, core))
                  for z in range(ring) for xy in range(nxy) for core in range(2)]
    line_groups = [[device(z, xy, core) for z in range(ring) for core in range(2)] for xy in range(nxy)]
    plane_groups = [[zh * nxy + xy for xy in range(nxy)] for zh in range(nzh)]
    coarse_matrix = coarsening()

    def swap_core(value):
        return lax.ppermute(value, "seq", core_pairs)

    def per_device(tokens, grad_out, stacked):
        seq = lax.axis_index("seq")
        zl = seq >> 1
        core = seq & 1
        first = core == 0

        def ordered(mine, other, axis):
            return jnp.where(first, jnp.concatenate([mine, other], axis), jnp.concatenate([other, mine], axis))

        both = ("dp", "seq")
        shard = stacked.reshape(64, 4, 2, 256).transpose(0, 2, 1, 3).reshape(64, 2048)
        shard_got = swap_core(shard)
        w0 = ordered(shard, shard_got, 0)
        r1 = lax.ppermute(w0, both, ring_pairs)
        r2 = lax.ppermute(r1, both, ring_pairs)
        r3 = lax.ppermute(r2, both, ring_pairs)
        r4 = lax.ppermute(lax.dynamic_slice(r3, (core * 64, 0), (64, 2048)), both, ring_pairs)

        def other_columns(value):
            return lax.dynamic_slice(value, (0, (1 - core) * 1024), (value.shape[0], 1024))

        x12 = swap_core(jnp.concatenate([other_columns(r1), other_columns(r2)], 0))
        x34 = swap_core(jnp.concatenate([other_columns(r3), other_columns(r4)], 0))

        own = jnp.concatenate([tokens[0], grad_out[0]], axis=0)
        own, _ = lax.optimization_barrier((own, shard_got))
        got = swap_core(own)
        chip_tokens = ordered(own[0:128], got[0:128], 0)
        chip_grads = ordered(own[128:256], got[128:256], 0)
        matrix = jnp.asarray(coarse_matrix, BF)
        half_tokens = lax.dynamic_slice(chip_tokens, (0, core * 512), (256, 512))
        coarse = nn(matrix, half_tokens).astype(BF)
        c1, c2, c3 = coarse[0:128], coarse[128:192], coarse[192:224]
        t3, _ = lax.optimization_barrier((lax.ppermute(c3, "seq", chip_swap(2)), r1))
        second, _ = lax.optimization_barrier((lax.ppermute(jnp.concatenate([c2, t3], 0), "seq", chip_swap(1)), r2))
        held = jnp.concatenate([second[0:64], t3, second[64:96]], 0)
        third = lax.ppermute(jnp.concatenate([c1, held], 0), "seq", chip_swap(0))
        half_set = jnp.concatenate([held, third], 0)
        rest = ordered(half_set, swap_core(half_set), 1)
        token_set = jnp.concatenate([chip_tokens, rest], 0)

        position = jnp.stack([zl, core]).astype(jnp.int32)
        (weight, part, layer_own, layer_send, dquery, grad_own, grad_keep, grad_send) = run_layer(
            nx, ny, position, token_set, token_set.T, chip_grads, chip_grads.T,
            w0, r1, r2, r3, r4, x12, x34)

        if nxy > 1:
            pieces = lax.all_to_all(part, "dp", 0, 0, axis_index_groups=plane_groups, tiled=True)
        else:
            pieces = part
        plane_sum = jnp.sum(pieces.astype(F32), axis=0).astype(BF)
        twice = jnp.concatenate([plane_sum] * nzh, axis=0)
        columns = lax.all_to_all(twice, both, 0, 0, axis_index_groups=line_groups, tiled=True)
        rows, cols = 64 // nx, 1024 // ny
        line_sum = jnp.sum(columns.astype(F32).reshape(ring, 2, rows, cols), axis=0).astype(BF)
        spread = jnp.broadcast_to(line_sum[None], (nxy, 2, rows, cols))
        if nxy > 1:
            spread = lax.all_to_all(spread, "dp", 0, 0, axis_index_groups=plane_groups, tiled=True)
        slots = 4 // ny
        full = spread.reshape(nx, ny, 2, rows, slots, 256).transpose(0, 3, 1, 4, 2, 5).reshape(64, 4, 512)
        total = 128 * seq_count * dp_count
        grad_weights = full.astype(F32) * (1.0 / math.sqrt(total))

        layer_out = (layer_own + swap_core(layer_send).astype(F32)).astype(BF)

        b1 = lax.ppermute(grad_send, "seq", chip_swap(0))
        joined = grad_keep + b1[128:256].astype(F32)
        b2 = lax.ppermute(jnp.concatenate([joined[0:64], joined[96:128]], 0).astype(BF), "seq", chip_swap(1))
        b3 = lax.ppermute((joined[64:96] + b2[64:96].astype(F32)).astype(BF), "seq", chip_swap(2))
        returned = jnp.concatenate([b1[0:128], b2[0:64], b3], 0)
        dkv = (grad_own + nn(jnp.asarray(coarse_matrix.T, BF), returned)).astype(BF)
        back = jnp.concatenate([dquery, dkv], axis=1)
        partial = nt(back, weight[:, 0:768])
        mine = lax.dynamic_slice(partial, (core * 128, 0), (128, 1024))
        theirs = lax.dynamic_slice(partial, ((1 - core) * 128, 0), (128, 1024)).astype(BF)
        grad_tokens = (mine + swap_core(theirs).astype(F32)).astype(BF)
        return layer_out[None], grad_tokens[None], grad_weights

    return per_device


def solution(mesh):
    dp_count, seq_count = mesh.shape["dp"], mesh.shape["seq"]
    side = 4 if dp_count >= 16 else (2 if dp_count >= 4 else 1)
    specs = (P("dp", "seq", None), P("dp", "seq", None), P("seq", None, None))
    return jax.shard_map(
        make_device(side, side, dp_count, seq_count),
        mesh=mesh, in_specs=specs, out_specs=specs, check_vma=False)
```

```python
import functools
import math

import jax
import jax.numpy as jnp
import numpy as np
from jax import lax
from jax.experimental import pallas as pl
from jax.experimental.pallas import tpu as pltpu
from jax.sharding import PartitionSpec as P

HEAD = 64
LOG_TWO = math.log(2.0)
BF = jnp.bfloat16
F32 = jnp.float32

ROW_LEVELS = ((0, 256, 0), (256, 320, 2), (320, 384, 3), (384, 512, 1), (512, 576, 2), (576, 640, 3))


def nn(a, b):
    return lax.dot_general(a, b, (((1,), (0,)), ((), ())), preferred_element_type=F32)


def nt(a, b):
    return lax.dot_general(a, b, (((1,), (1,)), ((), ())), preferred_element_type=F32)


def layer_kernel(nx, ny, pos_ref, *refs):
    sources, refs = refs[:8], refs[8:]
    results, refs = refs[:8], refs[8:]
    staged, refs = refs[:8], refs[8:]
    (tok_s, tokt_s, g_s, gt_s, kv_s, kvt_s, qm_s, gm_s, gkv_s, attt_s, dqt_s, att_s, in_sem, w_sem, out_sem, part_sem) = refs
    tok, tokt, g, gt, n1, n2, n3, n4 = sources
    w_s, part_s, lown_s, lsend_s, dq_s, gown_s, gkeep_s, gsend_s = staged
    zl = pos_ref[0]
    core = pos_ref[1]
    even = lax.rem(zl + core, 2) == 0
    base = jnp.where(even, zl, zl + 7)
    turn = jnp.where(even, 2, -2)
    moves = []
    for piece, start in ((n1, base), (n2, base - turn), (n3, base + turn), (n4, base + 4)):
        for k in range(2):
            row = pl.multiple_of(lax.rem(start + k + 8, 8) * 128, 128)
            moves.append((piece.at[pl.ds(128 * k, 128), :], w_s.at[pl.ds(row, 128), :]))
    weight_copies = [pltpu.make_async_copy(src, dst, w_sem.at[i]) for i, (src, dst) in enumerate(moves)]
    inputs = [pltpu.make_async_copy(src, dst, in_sem.at[i])
              for i, (src, dst) in enumerate(((tok, tok_s), (g, g_s), (tokt, tokt_s), (gt, gt_s)))]
    for copy in inputs[:1] + weight_copies + inputs[1:]:
        copy.start()
    outputs = {i: pltpu.make_async_copy(staged[i], results[i], out_sem.at[i]) for i in (0, 2, 3, 4, 5, 6, 7)}
    inputs[0].wait()
    for copy in weight_copies:
        copy.wait()
    outputs[0].start()

    def project_keys(step, carry):
        row = pl.multiple_of(step * 128, 128)
        block = nn(tok_s[pl.ds(row, 128), :], w_s[:, 256:768])
        kv_s[pl.ds(row, 128), :] = block.astype(BF)
        kvt_s[:, pl.ds(row, 128)] = block.T.astype(BF)
        return carry

    lax.fori_loop(0, 5, project_keys, 0)
    queries = nn(tok_s[0:256, :], w_s[:, 0:256]) * 0.125
    inputs[1].wait()
    grads = nn(g_s[...], w_s[:, 768:1024])
    lane = lax.broadcasted_iota(jnp.int32, (256, 128), 1)
    for head in range(4):
        pair = (head // 2) * 128
        mine = (lane >= 64) if head % 2 else (lane < 64)
        qm_s[head] = jnp.where(mine, queries[:, pair:pair + 128], 0.0).astype(BF)
        gm_s[head] = jnp.where(mine, grads[:, pair:pair + 128], 0.0).astype(BF)

    for pair in range(2):
        kcol = pair * 128
        vcol = 256 + pair * 128
        key_grad = None
        value_grad = None
        for half in range(2):
            head = 2 * pair + half
            qm = qm_s[head]
            gm = gm_s[head]
            raw = nt(kv_s[:, kcol:kcol + 128], qm)
            scores = jnp.concatenate(
                [raw[lo:hi] + level * LOG_TWO if level else raw[lo:hi] for lo, hi, level in ROW_LEVELS], axis=0)
            exponent = jnp.exp(scores - jnp.max(scores, axis=0, keepdims=True))
            weights = exponent * (1.0 / jnp.sum(exponent, axis=0, keepdims=True))
            low = weights.astype(BF)
            dprobs = nt(kv_s[:, vcol:vcol + 128], gm)
            rowdot = jnp.sum(weights * dprobs, axis=0, keepdims=True)
            dscore = (weights * (dprobs - rowdot)).astype(BF)
            rows = slice(head * 64, head * 64 + 64)
            attt_s[rows, :] = nn(kvt_s[256 + head * 64:320 + head * 64, :], low)
            dqt_s[rows, :] = nn(kvt_s[rows, :], dscore) * 0.125
            new_key = nn(dscore, qm)
            new_value = nn(low, gm)
            key_grad = new_key if key_grad is None else key_grad + new_key
            value_grad = new_value if value_grad is None else value_grad + new_value
        for col, grad in ((kcol, key_grad), (vcol, value_grad)):
            where = slice(col, col + 128)
            gown_s[:, where] = grad[0:256]
            gkeep_s[:, where] = grad[256:384]
            gkv_s[:, where] = grad.astype(BF)

    gsend_s[...] = gkv_s[384:640, :]
    dq_s[...] = dqt_s[...].T.astype(BF)
    attended = attt_s[...].T.astype(BF)
    att_s[0] = attended[0:128]
    att_s[1] = attended[128:256]
    for index in (4, 5, 6, 7):
        outputs[index].start()

    x_rows = 64 // nx
    y_cols = 1024 // ny
    inputs[2].wait()
    inputs[3].wait()

    def part_copy(step):
        where = pl.ds(2 * step, 2)
        return pltpu.make_async_copy(part_s.at[:, where], results[1].at[:, where], part_sem.at[step])

    def grad_rows(step, carry):
        rows = pl.ds(pl.multiple_of(step * 128, 128), 128)
        lhs = tokt_s[rows, :]
        att_all = jnp.concatenate([att_s[0], att_s[1]], axis=0)
        block = jnp.concatenate(
            [nn(lhs[:, 0:256], dq_s[...]).astype(BF), nn(lhs, gkv_s[...]).astype(BF),
             nn(gt_s[rows, :], att_all).astype(BF)], axis=1)
        for side in range(2):
            for x in range(nx):
                for y in range(ny):
                    part_s[x * ny + y, 2 * step + side] = block[
                        side * 64 + x * x_rows:side * 64 + (x + 1) * x_rows, y * y_cols:(y + 1) * y_cols]
        part_copy(step).start()
        return carry

    lax.fori_loop(0, 8, grad_rows, 0)
    lown_s[...] = nt(att_s[core], w_s[:, 768:1024])
    lsend_s[...] = nt(att_s[1 - core], w_s[:, 768:1024]).astype(BF)
    outputs[2].start()
    outputs[3].start()
    for step in range(8):
        part_copy(step).wait()
    for index in (0, 2, 3, 4, 5, 6, 7):
        outputs[index].wait()


def run_layer(nx, ny, *operands):
    anywhere = pl.BlockSpec(memory_space=pl.ANY)
    smem = pl.BlockSpec(memory_space=pltpu.SMEM)
    results = (
        ((1024, 1024), BF),
        ((nx * ny, 16, 64 // nx, 1024 // ny), BF),
        ((128, 1024), F32),
        ((128, 1024), BF),
        ((256, 256), BF),
        ((256, 512), F32),
        ((128, 512), F32),
        ((256, 512), BF),
    )
    return pl.pallas_call(
        functools.partial(layer_kernel, nx, ny),
        out_shape=tuple(jax.ShapeDtypeStruct(*result) for result in results),
        in_specs=[smem] + [anywhere] * (len(operands) - 1),
        out_specs=tuple([anywhere] * len(results)),
        scratch_shapes=[pltpu.VMEM(*result) for result in results] + [
            pltpu.VMEM((640, 1024), BF),
            pltpu.VMEM((1024, 640), BF),
            pltpu.VMEM((256, 1024), BF),
            pltpu.VMEM((1024, 256), BF),
            pltpu.VMEM((640, 512), BF),
            pltpu.VMEM((512, 640), BF),
            pltpu.VMEM((4, 256, 128), BF),
            pltpu.VMEM((4, 256, 128), BF),
            pltpu.VMEM((640, 512), BF),
            pltpu.VMEM((256, 256), F32),
            pltpu.VMEM((256, 256), F32),
            pltpu.VMEM((2, 128, 256), BF),
            pltpu.SemaphoreType.DMA((4,)),
            pltpu.SemaphoreType.DMA((8,)),
            pltpu.SemaphoreType.DMA((8,)),
            pltpu.SemaphoreType.DMA((8,)),
        ],
        compiler_params=pltpu.CompilerParams(vmem_limit_bytes=60 * 1024 * 1024),
        cost_estimate=pl.CostEstimate(flops=3_500_000_000, bytes_accessed=14_000_000, transcendentals=700_000),
    )(*operands)


def coarsening():
    matrix = np.zeros((224, 256), np.float32)
    base = 0
    for level in (1, 2, 3):
        for row in range(256 >> level):
            matrix[base + row, row << level:(row + 1) << level] = 0.5 ** level
        base += 256 >> level
    return matrix


def make_device(nx, ny, dp_count, seq_count):
    nxy = nx * ny
    nzh = dp_count // nxy
    ring = nzh * 8
    core_pairs = [(i, i ^ 1) for i in range(seq_count)]

    def chip_swap(bit):
        return [(i, i ^ (2 << bit)) for i in range(seq_count)]

    def device(z, xy, core):
        return ((z // 8) * nxy + xy) * seq_count + (z % 8) * 2 + core

    def swaps(turn):
        return [(device((z + 1 if (z + core + turn) % 2 == 0 else z - 1) % ring, xy, core), device(z, xy, core))
                for z in range(ring) for xy in range(nxy) for core in range(2)]

    swap_even, swap_odd = swaps(0), swaps(1)
    quad_groups = [[4 * quad + i for i in range(4)] for quad in range(seq_count // 4)]
    line_groups = [[(zh * nxy + xy) * seq_count + 4 * quad + i for zh in range(nzh) for quad in range(4)]
                   for xy in range(nxy) for i in range(4)]
    plane_groups = [[zh * nxy + xy for xy in range(nxy)] for zh in range(nzh)]
    coarse_matrix = coarsening()

    def swap_core(value):
        return lax.ppermute(value, "seq", core_pairs)

    def per_device(tokens, grad_out, stacked):
        seq = lax.axis_index("seq")
        zl = seq >> 1
        core = seq & 1
        first = core == 0

        def ordered(mine, other, axis):
            return jnp.where(first, jnp.concatenate([mine, other], axis), jnp.concatenate([other, mine], axis))

        both = ("dp", "seq")
        shard = stacked.reshape(64, 4, 2, 256)
        keep = lax.dynamic_index_in_dim(shard, core, 2, False).reshape(64, 1024)
        give = lax.dynamic_index_in_dim(shard, 1 - core, 2, False).reshape(64, 1024)
        shard_got = swap_core(give)
        w0 = ordered(keep, shard_got, 0)
        w1 = lax.ppermute(w0, both, swap_even)
        even = (zl + core) & 1 == 0
        n1 = jnp.where(even, jnp.concatenate([w0, w1], 0), jnp.concatenate([w1, w0], 0))
        n2 = lax.ppermute(n1, both, swap_odd)
        n3 = lax.ppermute(n2, both, swap_even)
        n4 = lax.ppermute(n3, both, swap_odd)

        own = jnp.concatenate([tokens[0], grad_out[0]], axis=0)
        own, _ = lax.optimization_barrier((own, shard_got))
        got = swap_core(own)
        chip_tokens = ordered(own[0:128], got[0:128], 0)
        chip_grads = ordered(own[128:256], got[128:256], 0)
        matrix = jnp.asarray(coarse_matrix, BF)
        half_tokens = lax.dynamic_slice(chip_tokens, (0, core * 512), (256, 512))
        coarse = nn(matrix, half_tokens).astype(BF)
        c1, c2, c3 = coarse[0:128], coarse[128:192], coarse[192:224]
        t3 = lax.ppermute(c3, "seq", chip_swap(2))
        second = lax.ppermute(jnp.concatenate([c2, t3], 0), "seq", chip_swap(1))
        held = jnp.concatenate([second[0:64], t3, second[64:96]], 0)
        third = lax.ppermute(jnp.concatenate([c1, held], 0), "seq", chip_swap(0))
        half_set = jnp.concatenate([held, third], 0)
        rest = ordered(half_set, swap_core(half_set), 1)
        token_set = jnp.concatenate([chip_tokens, rest], 0)

        position = jnp.stack([zl, core]).astype(jnp.int32)
        (weight, part, layer_own, layer_send, dquery, grad_own, grad_keep, grad_send) = run_layer(
            nx, ny, position, token_set, token_set.T, chip_grads, chip_grads.T,
            n1, n2, n3, n4)

        if nxy > 1:
            pieces = lax.all_to_all(part, "dp", 0, 0, axis_index_groups=plane_groups, tiled=True)
        else:
            pieces = part
        plane_sum = jnp.sum(pieces.astype(F32), axis=0).astype(BF)
        rows, cols = 64 // nx, 1024 // ny
        by_chip = plane_sum.reshape(4, 4, rows, cols).transpose(1, 0, 2, 3)
        by_chip = lax.all_to_all(by_chip, "seq", 0, 0, axis_index_groups=quad_groups, tiled=True)
        quad_sum = jnp.sum(by_chip.astype(F32).reshape(2, 2, 4, rows, cols), axis=0).astype(BF)
        by_quad = quad_sum.transpose(1, 0, 2, 3)
        by_quad = lax.all_to_all(jnp.concatenate([by_quad] * nzh, axis=0), both, 0, 0,
                                 axis_index_groups=line_groups, tiled=True)
        line_sum = jnp.sum(by_quad.astype(F32), axis=0).astype(BF)
        spread = jnp.broadcast_to(line_sum[None], (nxy, 2, rows, cols))
        if nxy > 1:
            spread = lax.all_to_all(spread, "dp", 0, 0, axis_index_groups=plane_groups, tiled=True)
        slots = 4 // ny
        full = spread.reshape(nx, ny, 2, rows, slots, 256).transpose(0, 3, 1, 4, 2, 5).reshape(64, 4, 512)
        total = 128 * seq_count * dp_count
        grad_weights = full.astype(F32) * (1.0 / math.sqrt(total))

        layer_out = (layer_own + swap_core(layer_send).astype(F32)).astype(BF)

        b1 = lax.ppermute(grad_send, "seq", chip_swap(0))
        joined = grad_keep + b1[128:256].astype(F32)
        b2 = lax.ppermute(jnp.concatenate([joined[0:64], joined[96:128]], 0).astype(BF), "seq", chip_swap(1))
        b3 = lax.ppermute((joined[64:96] + b2[64:96].astype(F32)).astype(BF), "seq", chip_swap(2))
        returned = jnp.concatenate([b1[0:128], b2[0:64], b3], 0)
        dkv = (grad_own + nn(jnp.asarray(coarse_matrix.T, BF), returned)).astype(BF)
        back = jnp.concatenate([dquery, dkv], axis=1)
        partial = nt(back, weight[:, 0:768])
        mine = lax.dynamic_slice(partial, (core * 128, 0), (128, 1024))
        theirs = lax.dynamic_slice(partial, ((1 - core) * 128, 0), (128, 1024)).astype(BF)
        grad_tokens = (mine + swap_core(theirs).astype(F32)).astype(BF)
        return layer_out[None], grad_tokens[None], grad_weights

    return per_device


def solution(mesh):
    dp_count, seq_count = mesh.shape["dp"], mesh.shape["seq"]
    side = 4 if dp_count >= 16 else (2 if dp_count >= 4 else 1)
    specs = (P("dp", "seq", None), P("dp", "seq", None), P("seq", None, None))
    return jax.shard_map(
        make_device(side, side, dp_count, seq_count),
        mesh=mesh, in_specs=specs, out_specs=specs, check_vma=False)
```

```python
import functools
import math

import jax
import jax.numpy as jnp
import numpy as np
from jax import lax
from jax.experimental import pallas as pl
from jax.experimental.pallas import tpu as pltpu
from jax.sharding import PartitionSpec as P

HEAD = 64
LOG_TWO = math.log(2.0)
BF = jnp.bfloat16
F32 = jnp.float32

ROW_LEVELS = ((0, 256, 0), (256, 320, 2), (320, 384, 3), (384, 512, 1), (512, 576, 2), (576, 640, 3))


def nn(a, b):
    return lax.dot_general(a, b, (((1,), (0,)), ((), ())), preferred_element_type=F32)


def nt(a, b):
    return lax.dot_general(a, b, (((1,), (1,)), ((), ())), preferred_element_type=F32)


def layer_kernel(nx, ny, pos_ref, *refs):
    sources, refs = refs[:12], refs[12:]
    results, refs = refs[:8], refs[8:]
    staged, refs = refs[:8], refs[8:]
    (tok_s, tokt_s, g_s, gt_s, kv_s, kvt_s, qm_s, gm_s, gkv_s, attt_s, dqt_s, att_s, in_sem, w_sem, out_sem, part_sem) = refs
    own, ownt, mine, minet, other, othert, g, gt, n1, n2, n3, n4 = sources
    w_s, part_s, lown_s, lsend_s, dq_s, gown_s, gkeep_s, gsend_s = staged
    zl = pos_ref[0]
    core = pos_ref[1]
    even = lax.rem(zl + core, 2) == 0
    base = jnp.where(even, zl, zl + 7)
    turn = jnp.where(even, 2, -2)
    moves = []
    for piece, start in ((n1, base), (n2, base - turn), (n3, base + turn), (n4, base + 4)):
        for k in range(2):
            row = pl.multiple_of(lax.rem(start + k + 8, 8) * 128, 128)
            moves.append((piece.at[pl.ds(128 * k, 128), :], w_s.at[pl.ds(row, 128), :]))
    weight_copies = [pltpu.make_async_copy(src, dst, w_sem.at[i]) for i, (src, dst) in enumerate(moves)]
    here = pl.ds(pl.multiple_of(core * 512, 512), 512)
    there = pl.ds(pl.multiple_of((1 - core) * 512, 512), 512)
    pairs = (
        (own, tok_s.at[pl.ds(0, 256), :]),
        (mine, tok_s.at[pl.ds(256, 384), here]),
        (other, tok_s.at[pl.ds(256, 384), there]),
        (g, g_s),
        (ownt, tokt_s.at[:, pl.ds(0, 256)]),
        (minet, tokt_s.at[here, pl.ds(256, 384)]),
        (othert, tokt_s.at[there, pl.ds(256, 384)]),
        (gt, gt_s),
    )
    inputs = [pltpu.make_async_copy(src, dst, in_sem.at[i]) for i, (src, dst) in enumerate(pairs)]
    for copy in inputs[:3] + weight_copies + inputs[3:]:
        copy.start()
    outputs = {i: pltpu.make_async_copy(staged[i], results[i], out_sem.at[i]) for i in (0, 2, 3, 4, 5, 6, 7)}
    for copy in inputs[:3] + weight_copies:
        copy.wait()
    outputs[0].start()

    def project_keys(step, carry):
        row = pl.multiple_of(step * 128, 128)
        block = nn(tok_s[pl.ds(row, 128), :], w_s[:, 256:768])
        kv_s[pl.ds(row, 128), :] = block.astype(BF)
        kvt_s[:, pl.ds(row, 128)] = block.T.astype(BF)
        return carry

    lax.fori_loop(0, 5, project_keys, 0)
    queries = nn(tok_s[0:256, :], w_s[:, 0:256]) * 0.125
    inputs[3].wait()
    grads = nn(g_s[...], w_s[:, 768:1024])
    lane = lax.broadcasted_iota(jnp.int32, (256, 128), 1)
    for head in range(4):
        pair = (head // 2) * 128
        mine = (lane >= 64) if head % 2 else (lane < 64)
        qm_s[head] = jnp.where(mine, queries[:, pair:pair + 128], 0.0).astype(BF)
        gm_s[head] = jnp.where(mine, grads[:, pair:pair + 128], 0.0).astype(BF)

    for pair in range(2):
        kcol = pair * 128
        vcol = 256 + pair * 128
        key_grad = None
        value_grad = None
        for half in range(2):
            head = 2 * pair + half
            qm = qm_s[head]
            gm = gm_s[head]
            raw = nt(kv_s[:, kcol:kcol + 128], qm)
            scores = jnp.concatenate(
                [raw[lo:hi] + level * LOG_TWO if level else raw[lo:hi] for lo, hi, level in ROW_LEVELS], axis=0)
            exponent = jnp.exp(scores - jnp.max(scores, axis=0, keepdims=True))
            weights = exponent * (1.0 / jnp.sum(exponent, axis=0, keepdims=True))
            low = weights.astype(BF)
            dprobs = nt(kv_s[:, vcol:vcol + 128], gm)
            rowdot = jnp.sum(weights * dprobs, axis=0, keepdims=True)
            dscore = (weights * (dprobs - rowdot)).astype(BF)
            rows = slice(head * 64, head * 64 + 64)
            attt_s[rows, :] = nn(kvt_s[256 + head * 64:320 + head * 64, :], low)
            dqt_s[rows, :] = nn(kvt_s[rows, :], dscore) * 0.125
            new_key = nn(dscore, qm)
            new_value = nn(low, gm)
            key_grad = new_key if key_grad is None else key_grad + new_key
            value_grad = new_value if value_grad is None else value_grad + new_value
        for col, grad in ((kcol, key_grad), (vcol, value_grad)):
            where = slice(col, col + 128)
            gown_s[:, where] = grad[0:256]
            gkeep_s[:, where] = grad[256:384]
            gkv_s[:, where] = grad.astype(BF)

    gsend_s[...] = gkv_s[384:640, :]
    dq_s[...] = dqt_s[...].T.astype(BF)
    attended = attt_s[...].T.astype(BF)
    att_s[0] = attended[0:128]
    att_s[1] = attended[128:256]
    for index in (4, 5, 6, 7):
        outputs[index].start()

    x_rows = 64 // nx
    y_cols = 1024 // ny
    for copy in inputs[4:]:
        copy.wait()

    def part_copy(low):
        where = pl.ds(8 * low, 8)
        return pltpu.make_async_copy(part_s.at[:, where], results[1].at[:, where], part_sem.at[low])

    def grad_rows(low, quad, carry):
        rows = pl.ds(pl.multiple_of((2 * quad + low) * 128, 128), 128)
        lhs = tokt_s[rows, :]
        att_all = jnp.concatenate([att_s[0], att_s[1]], axis=0)
        block = jnp.concatenate(
            [nn(lhs[:, 0:256], dq_s[...]).astype(BF), nn(lhs, gkv_s[...]).astype(BF),
             nn(gt_s[rows, :], att_all).astype(BF)], axis=1)
        for side in range(2):
            for x in range(nx):
                for y in range(ny):
                    part_s[x * ny + y, (2 * low + side) * 4 + quad] = block[
                        side * 64 + x * x_rows:side * 64 + (x + 1) * x_rows, y * y_cols:(y + 1) * y_cols]
        return carry

    for low in range(2):
        lax.fori_loop(0, 4, functools.partial(grad_rows, low), 0)
        part_copy(low).start()
    lown_s[...] = nt(att_s[core], w_s[:, 768:1024])
    lsend_s[...] = nt(att_s[1 - core], w_s[:, 768:1024]).astype(BF)
    outputs[2].start()
    outputs[3].start()
    for low in range(2):
        part_copy(low).wait()
    for index in (0, 2, 3, 4, 5, 6, 7):
        outputs[index].wait()


def run_layer(nx, ny, *operands):
    anywhere = pl.BlockSpec(memory_space=pl.ANY)
    smem = pl.BlockSpec(memory_space=pltpu.SMEM)
    results = (
        ((1024, 1024), BF),
        ((nx * ny, 16, 64 // nx, 1024 // ny), BF),
        ((128, 1024), F32),
        ((128, 1024), BF),
        ((256, 256), BF),
        ((256, 512), F32),
        ((128, 512), F32),
        ((256, 512), BF),
    )
    return pl.pallas_call(
        functools.partial(layer_kernel, nx, ny),
        out_shape=tuple(jax.ShapeDtypeStruct(*result) for result in results),
        in_specs=[smem] + [anywhere] * (len(operands) - 1),
        out_specs=tuple([anywhere] * len(results)),
        scratch_shapes=[pltpu.VMEM(*result) for result in results] + [
            pltpu.VMEM((640, 1024), BF),
            pltpu.VMEM((1024, 640), BF),
            pltpu.VMEM((256, 1024), BF),
            pltpu.VMEM((1024, 256), BF),
            pltpu.VMEM((640, 512), BF),
            pltpu.VMEM((512, 640), BF),
            pltpu.VMEM((4, 256, 128), BF),
            pltpu.VMEM((4, 256, 128), BF),
            pltpu.VMEM((640, 512), BF),
            pltpu.VMEM((256, 256), F32),
            pltpu.VMEM((256, 256), F32),
            pltpu.VMEM((2, 128, 256), BF),
            pltpu.SemaphoreType.DMA((8,)),
            pltpu.SemaphoreType.DMA((8,)),
            pltpu.SemaphoreType.DMA((8,)),
            pltpu.SemaphoreType.DMA((2,)),
        ],
        compiler_params=pltpu.CompilerParams(vmem_limit_bytes=60 * 1024 * 1024),
        cost_estimate=pl.CostEstimate(flops=3_500_000_000, bytes_accessed=14_000_000, transcendentals=700_000),
    )(*operands)


def coarsening():
    matrix = np.zeros((224, 256), np.float32)
    base = 0
    for level in (1, 2, 3):
        for row in range(256 >> level):
            matrix[base + row, row << level:(row + 1) << level] = 0.5 ** level
        base += 256 >> level
    return matrix


def make_device(nx, ny, dp_count, seq_count):
    nxy = nx * ny
    nzh = dp_count // nxy
    ring = nzh * 8
    core_pairs = [(i, i ^ 1) for i in range(seq_count)]

    def chip_swap(bit):
        return [(i, i ^ (2 << bit)) for i in range(seq_count)]

    def device(z, xy, core):
        return ((z // 8) * nxy + xy) * seq_count + (z % 8) * 2 + core

    def swaps(turn):
        return [(device((z + 1 if (z + core + turn) % 2 == 0 else z - 1) % ring, xy, core), device(z, xy, core))
                for z in range(ring) for xy in range(nxy) for core in range(2)]

    swap_even, swap_odd = swaps(0), swaps(1)
    quad_groups = [[4 * quad + i for i in range(4)] for quad in range(seq_count // 4)]
    line_groups = [[(zh * nxy + xy) * seq_count + 4 * quad + i for zh in range(nzh) for quad in range(4)]
                   for xy in range(nxy) for i in range(4)]
    plane_groups = [[zh * nxy + xy for xy in range(nxy)] for zh in range(nzh)]
    coarse_matrix = coarsening()

    def swap_core(value):
        return lax.ppermute(value, "seq", core_pairs)

    def per_device(tokens, grad_out, stacked):
        seq = lax.axis_index("seq")
        zl = seq >> 1
        core = seq & 1
        first = core == 0

        def ordered(mine, other, axis):
            return jnp.where(first, jnp.concatenate([mine, other], axis), jnp.concatenate([other, mine], axis))

        both = ("dp", "seq")
        def shard_half(which):
            return lax.dynamic_slice(stacked, (0, 0, which * 256), (64, 4, 256)).reshape(64, 1024)

        keep, give = shard_half(core), shard_half(1 - core)
        shard_got = swap_core(give)
        w0 = ordered(keep, shard_got, 0)
        w1 = lax.ppermute(w0, both, swap_even)
        even = (zl + core) & 1 == 0
        n1 = jnp.where(even, jnp.concatenate([w0, w1], 0), jnp.concatenate([w1, w0], 0))

        own = jnp.concatenate([tokens[0], grad_out[0]], axis=0)
        got = swap_core(own)
        chip_tokens = ordered(own[0:128], got[0:128], 0)
        chip_grads = ordered(own[128:256], got[128:256], 0)
        matrix = jnp.asarray(coarse_matrix, BF)
        half_tokens = lax.dynamic_slice(chip_tokens, (0, core * 512), (256, 512))
        coarse = nn(matrix, half_tokens).astype(BF)
        n1, coarse = lax.optimization_barrier((n1, coarse))
        c1, c2, c3 = coarse[0:128], coarse[128:192], coarse[192:224]
        n2 = lax.ppermute(n1, both, swap_odd)
        t3 = lax.ppermute(c3, "seq", chip_swap(2))
        n2, t3 = lax.optimization_barrier((n2, t3))
        n3 = lax.ppermute(n2, both, swap_even)
        second = lax.ppermute(jnp.concatenate([c2, t3], 0), "seq", chip_swap(1))
        n3, second = lax.optimization_barrier((n3, second))
        n4 = lax.ppermute(n3, both, swap_odd)
        held = jnp.concatenate([second[0:64], t3, second[64:96]], 0)
        third = lax.ppermute(jnp.concatenate([c1, held], 0), "seq", chip_swap(0))
        half_set = jnp.concatenate([held, third], 0)
        other_set = swap_core(half_set)

        position = jnp.stack([zl, core]).astype(jnp.int32)
        (weight, part, layer_own, layer_send, dquery, grad_own, grad_keep, grad_send) = run_layer(
            nx, ny, position, chip_tokens, chip_tokens.T, half_set, half_set.T, other_set, other_set.T,
            chip_grads, chip_grads.T,
            n1, n2, n3, n4)

        if nxy > 1:
            pieces = lax.all_to_all(part, "dp", 0, 0, axis_index_groups=plane_groups, tiled=True)
        else:
            pieces = part
        plane_sum = jnp.sum(pieces.astype(F32), axis=0).astype(BF)
        rows, cols = 64 // nx, 1024 // ny
        by_chip = plane_sum.reshape(4, 4, rows, cols)
        by_chip = lax.all_to_all(by_chip, "seq", 0, 0, axis_index_groups=quad_groups, tiled=True)
        quad_sum = jnp.sum(by_chip.astype(F32).reshape(2, 2, 4, rows, cols), axis=0).astype(BF)
        by_quad = quad_sum.transpose(1, 0, 2, 3)
        by_quad = lax.all_to_all(jnp.concatenate([by_quad] * nzh, axis=0), both, 0, 0,
                                 axis_index_groups=line_groups, tiled=True)
        line_sum = jnp.sum(by_quad.astype(F32), axis=0).astype(BF)
        spread = jnp.broadcast_to(line_sum[None], (nxy, 2, rows, cols))
        if nxy > 1:
            spread = lax.all_to_all(spread, "dp", 0, 0, axis_index_groups=plane_groups, tiled=True)
        slots = 4 // ny
        full = spread.reshape(nx, ny, 2, rows, slots, 256).transpose(0, 3, 1, 4, 2, 5).reshape(64, 4, 512)
        total = 128 * seq_count * dp_count
        grad_weights = full.astype(F32) * (1.0 / math.sqrt(total))

        layer_out = (layer_own + swap_core(layer_send).astype(F32)).astype(BF)

        b1 = lax.ppermute(grad_send, "seq", chip_swap(0))
        joined = grad_keep + b1[128:256].astype(F32)
        b2 = lax.ppermute(jnp.concatenate([joined[0:64], joined[96:128]], 0).astype(BF), "seq", chip_swap(1))
        b3 = lax.ppermute((joined[64:96] + b2[64:96].astype(F32)).astype(BF), "seq", chip_swap(2))
        returned = jnp.concatenate([b1[0:128], b2[0:64], b3], 0)
        dkv = (grad_own + nn(jnp.asarray(coarse_matrix.T, BF), returned)).astype(BF)
        back = jnp.concatenate([dquery, dkv], axis=1)
        partial = nt(back, weight[:, 0:768])
        mine = lax.dynamic_slice(partial, (core * 128, 0), (128, 1024))
        theirs = lax.dynamic_slice(partial, ((1 - core) * 128, 0), (128, 1024)).astype(BF)
        grad_tokens = (mine + swap_core(theirs).astype(F32)).astype(BF)
        return layer_out[None], grad_tokens[None], grad_weights

    return per_device


def solution(mesh):
    dp_count, seq_count = mesh.shape["dp"], mesh.shape["seq"]
    side = 4 if dp_count >= 16 else (2 if dp_count >= 4 else 1)
    specs = (P("dp", "seq", None), P("dp", "seq", None), P("seq", None, None))
    return jax.shard_map(
        make_device(side, side, dp_count, seq_count),
        mesh=mesh, in_specs=specs, out_specs=specs, check_vma=False)
```

```python
import functools
import math

import jax
import jax.numpy as jnp
import numpy as np
from jax import lax
from jax.experimental import pallas as pl
from jax.experimental.pallas import tpu as pltpu
from jax.sharding import PartitionSpec as P

HEAD = 64
LOG_TWO = math.log(2.0)
BF = jnp.bfloat16
F32 = jnp.float32

ROW_LEVELS = ((0, 256, 0), (256, 320, 2), (320, 384, 3), (384, 512, 1), (512, 576, 2), (576, 640, 3))


def nn(a, b):
    return lax.dot_general(a, b, (((1,), (0,)), ((), ())), preferred_element_type=F32)


def nt(a, b):
    return lax.dot_general(a, b, (((1,), (1,)), ((), ())), preferred_element_type=F32)


def layer_kernel(nx, ny, pos_ref, *refs):
    sources, refs = refs[:12], refs[12:]
    results, refs = refs[:8], refs[8:]
    staged, refs = refs[:8], refs[8:]
    (tok_s, tokt_s, g_s, gt_s, kv_s, kvt_s, qm_s, gm_s, gkv_s, attt_s, dqt_s, att_s, in_sem, w_sem, out_sem, part_sem) = refs
    own, ownt, mine, minet, other, othert, g, gt, n1, n2, n3, n4 = sources
    w_s, part_s, lown_s, lsend_s, dq_s, gown_s, gkeep_s, gsend_s = staged
    zl = pos_ref[0]
    core = pos_ref[1]
    even = lax.rem(zl + core, 2) == 0
    base = jnp.where(even, zl, zl + 7)
    turn = jnp.where(even, 2, -2)
    moves = []
    for piece, start in ((n1, base), (n2, base - turn), (n3, base + turn), (n4, base + 4)):
        for k in range(2):
            row = pl.multiple_of(lax.rem(start + k + 8, 8) * 128, 128)
            moves.append((piece.at[pl.ds(128 * k, 128), :], w_s.at[pl.ds(row, 128), :]))
    weight_copies = [pltpu.make_async_copy(src, dst, w_sem.at[i]) for i, (src, dst) in enumerate(moves)]
    here = pl.ds(pl.multiple_of(core * 512, 512), 512)
    there = pl.ds(pl.multiple_of((1 - core) * 512, 512), 512)
    pairs = (
        (own, tok_s.at[pl.ds(0, 256), :]),
        (mine, tok_s.at[pl.ds(256, 384), here]),
        (other, tok_s.at[pl.ds(256, 384), there]),
        (g, g_s),
        (ownt, tokt_s.at[:, pl.ds(0, 256)]),
        (minet, tokt_s.at[here, pl.ds(256, 384)]),
        (othert, tokt_s.at[there, pl.ds(256, 384)]),
        (gt, gt_s),
    )
    inputs = [pltpu.make_async_copy(src, dst, in_sem.at[i]) for i, (src, dst) in enumerate(pairs)]
    for copy in inputs[:3] + weight_copies + inputs[3:]:
        copy.start()
    outputs = {i: pltpu.make_async_copy(staged[i], results[i], out_sem.at[i]) for i in (0, 2, 3, 4, 5, 6, 7)}
    for copy in inputs[:3] + weight_copies:
        copy.wait()
    outputs[0].start()

    def project_keys(step, carry):
        row = pl.multiple_of(step * 128, 128)
        block = nn(tok_s[pl.ds(row, 128), :], w_s[:, 256:768])
        kv_s[pl.ds(row, 128), :] = block.astype(BF)
        kvt_s[:, pl.ds(row, 128)] = block.T.astype(BF)
        return carry

    lax.fori_loop(0, 5, project_keys, 0)
    queries = nn(tok_s[0:256, :], w_s[:, 0:256]) * 0.125
    inputs[3].wait()
    grads = nn(g_s[...], w_s[:, 768:1024])
    lane = lax.broadcasted_iota(jnp.int32, (256, 128), 1)
    for head in range(4):
        pair = (head // 2) * 128
        mine = (lane >= 64) if head % 2 else (lane < 64)
        qm_s[head] = jnp.where(mine, queries[:, pair:pair + 128], 0.0).astype(BF)
        gm_s[head] = jnp.where(mine, grads[:, pair:pair + 128], 0.0).astype(BF)

    for pair in range(2):
        kcol = pair * 128
        vcol = 256 + pair * 128
        key_grad = None
        value_grad = None
        for half in range(2):
            head = 2 * pair + half
            qm = qm_s[head]
            gm = gm_s[head]
            raw = nt(kv_s[:, kcol:kcol + 128], qm)
            scores = jnp.concatenate(
                [raw[lo:hi] + level * LOG_TWO if level else raw[lo:hi] for lo, hi, level in ROW_LEVELS], axis=0)
            exponent = jnp.exp(scores - jnp.max(scores, axis=0, keepdims=True))
            weights = exponent * (1.0 / jnp.sum(exponent, axis=0, keepdims=True))
            low = weights.astype(BF)
            dprobs = nt(kv_s[:, vcol:vcol + 128], gm)
            rowdot = jnp.sum(weights * dprobs, axis=0, keepdims=True)
            dscore = (weights * (dprobs - rowdot)).astype(BF)
            rows = slice(head * 64, head * 64 + 64)
            attt_s[rows, :] = nn(kvt_s[256 + head * 64:320 + head * 64, :], low)
            dqt_s[rows, :] = nn(kvt_s[rows, :], dscore) * 0.125
            new_key = nn(dscore, qm)
            new_value = nn(low, gm)
            key_grad = new_key if key_grad is None else key_grad + new_key
            value_grad = new_value if value_grad is None else value_grad + new_value
        for col, grad in ((kcol, key_grad), (vcol, value_grad)):
            where = slice(col, col + 128)
            gown_s[:, where] = grad[0:256]
            gkeep_s[:, where] = grad[256:384]
            gkv_s[:, where] = grad.astype(BF)

    gsend_s[...] = gkv_s[384:640, :]
    dq_s[...] = dqt_s[...].T.astype(BF)
    attended = attt_s[...].T.astype(BF)
    att_s[0] = attended[0:128]
    att_s[1] = attended[128:256]
    for index in (4, 5, 6, 7):
        outputs[index].start()

    x_rows = 64 // nx
    y_cols = 1024 // ny
    for copy in inputs[4:]:
        copy.wait()

    def part_copy(low):
        where = pl.ds(8 * low, 8)
        return pltpu.make_async_copy(part_s.at[:, where], results[1].at[:, where], part_sem.at[low])

    def grad_rows(low, quad, carry):
        rows = pl.ds(pl.multiple_of((2 * quad + low) * 128, 128), 128)
        lhs = tokt_s[rows, :]
        att_all = jnp.concatenate([att_s[0], att_s[1]], axis=0)
        block = jnp.concatenate(
            [nn(lhs[:, 0:256], dq_s[...]).astype(BF), nn(lhs, gkv_s[...]).astype(BF),
             nn(gt_s[rows, :], att_all).astype(BF)], axis=1)
        for side in range(2):
            for x in range(nx):
                for y in range(ny):
                    part_s[x * ny + y, (2 * low + side) * 4 + quad] = block[
                        side * 64 + x * x_rows:side * 64 + (x + 1) * x_rows, y * y_cols:(y + 1) * y_cols]
        return carry

    for low in range(2):
        lax.fori_loop(0, 4, functools.partial(grad_rows, low), 0)
        part_copy(low).start()
    lown_s[...] = nt(att_s[core], w_s[:, 768:1024])
    lsend_s[...] = nt(att_s[1 - core], w_s[:, 768:1024]).astype(BF)
    outputs[2].start()
    outputs[3].start()
    for low in range(2):
        part_copy(low).wait()
    for index in (0, 2, 3, 4, 5, 6, 7):
        outputs[index].wait()


def run_layer(nx, ny, *operands):
    anywhere = pl.BlockSpec(memory_space=pl.ANY)
    smem = pl.BlockSpec(memory_space=pltpu.SMEM)
    results = (
        ((1024, 1024), BF),
        ((nx * ny, 16, 64 // nx, 1024 // ny), BF),
        ((128, 1024), F32),
        ((128, 1024), BF),
        ((256, 256), BF),
        ((256, 512), F32),
        ((128, 512), F32),
        ((256, 512), BF),
    )
    return pl.pallas_call(
        functools.partial(layer_kernel, nx, ny),
        out_shape=tuple(jax.ShapeDtypeStruct(*result) for result in results),
        in_specs=[smem] + [anywhere] * (len(operands) - 1),
        out_specs=tuple([anywhere] * len(results)),
        scratch_shapes=[pltpu.VMEM(*result) for result in results] + [
            pltpu.VMEM((640, 1024), BF),
            pltpu.VMEM((1024, 640), BF),
            pltpu.VMEM((256, 1024), BF),
            pltpu.VMEM((1024, 256), BF),
            pltpu.VMEM((640, 512), BF),
            pltpu.VMEM((512, 640), BF),
            pltpu.VMEM((4, 256, 128), BF),
            pltpu.VMEM((4, 256, 128), BF),
            pltpu.VMEM((640, 512), BF),
            pltpu.VMEM((256, 256), F32),
            pltpu.VMEM((256, 256), F32),
            pltpu.VMEM((2, 128, 256), BF),
            pltpu.SemaphoreType.DMA((8,)),
            pltpu.SemaphoreType.DMA((8,)),
            pltpu.SemaphoreType.DMA((8,)),
            pltpu.SemaphoreType.DMA((2,)),
        ],
        compiler_params=pltpu.CompilerParams(vmem_limit_bytes=60 * 1024 * 1024),
        cost_estimate=pl.CostEstimate(flops=3_500_000_000, bytes_accessed=14_000_000, transcendentals=700_000),
    )(*operands)


def coarsening():
    matrix = np.zeros((224, 256), np.float32)
    base = 0
    for level in (1, 2, 3):
        for row in range(256 >> level):
            matrix[base + row, row << level:(row + 1) << level] = 0.5 ** level
        base += 256 >> level
    return matrix


def make_device(nx, ny, dp_count, seq_count):
    nxy = nx * ny
    nzh = dp_count // nxy
    ring = nzh * 8
    core_pairs = [(i, i ^ 1) for i in range(seq_count)]

    def chip_swap(bit):
        return [(i, i ^ (2 << bit)) for i in range(seq_count)]

    def device(z, xy, core):
        return ((z // 8) * nxy + xy) * seq_count + (z % 8) * 2 + core

    def swaps(turn):
        return [(device((z + 1 if (z + core + turn) % 2 == 0 else z - 1) % ring, xy, core), device(z, xy, core))
                for z in range(ring) for xy in range(nxy) for core in range(2)]

    swap_even, swap_odd = swaps(0), swaps(1)
    quad_groups = [[4 * quad + i for i in range(4)] for quad in range(seq_count // 4)]
    line_groups = [[(zh * nxy + xy) * seq_count + 4 * quad + i for zh in range(nzh) for quad in range(4)]
                   for xy in range(nxy) for i in range(4)]
    plane_groups = [[zh * nxy + xy for xy in range(nxy)] for zh in range(nzh)]
    coarse_matrix = coarsening()

    def swap_core(value):
        return lax.ppermute(value, "seq", core_pairs)

    def per_device(tokens, grad_out, stacked):
        seq = lax.axis_index("seq")
        zl = seq >> 1
        core = seq & 1
        first = core == 0

        def ordered(mine, other, axis):
            return jnp.where(first, jnp.concatenate([mine, other], axis), jnp.concatenate([other, mine], axis))

        both = ("dp", "seq")
        def shard_half(which):
            return lax.dynamic_slice(stacked, (0, 0, which * 256), (64, 4, 256)).reshape(64, 1024)

        keep, give = shard_half(core), shard_half(1 - core)
        shard_got = swap_core(give)
        w0 = ordered(keep, shard_got, 0)

        own = jnp.concatenate([tokens[0], grad_out[0]], axis=0)
        got = swap_core(own)
        chip_tokens = ordered(own[0:128], got[0:128], 0)
        chip_grads = ordered(own[128:256], got[128:256], 0)
        matrix = jnp.asarray(coarse_matrix, BF)
        half_tokens = lax.dynamic_slice(chip_tokens, (0, core * 512), (256, 512))
        coarse = nn(matrix, half_tokens).astype(BF)
        c1, c2, c3 = coarse[0:128], coarse[128:192], coarse[192:224]

        even = (zl + core) & 1 == 0
        t3 = lax.ppermute(c3, "seq", chip_swap(2))
        second = lax.ppermute(jnp.concatenate([c2, t3], 0), "seq", chip_swap(1))
        held = jnp.concatenate([second[0:64], t3, second[64:96]], 0)
        w0, held, to_third = lax.optimization_barrier((w0, held, jnp.concatenate([c1, held], 0)))
        third = lax.ppermute(to_third, "seq", chip_swap(0))
        w1 = lax.ppermute(w0, both, swap_even)
        half_set = jnp.concatenate([held, third], 0)
        w1, half_set = lax.optimization_barrier((w1, half_set))
        n1 = jnp.where(even, jnp.concatenate([w0, w1], 0), jnp.concatenate([w1, w0], 0))
        n2 = lax.ppermute(n1, both, swap_odd)
        n3 = lax.ppermute(n2, both, swap_even)
        n4 = lax.ppermute(n3, both, swap_odd)
        other_set = swap_core(half_set)

        position = jnp.stack([zl, core]).astype(jnp.int32)
        (weight, part, layer_own, layer_send, dquery, grad_own, grad_keep, grad_send) = run_layer(
            nx, ny, position, chip_tokens, chip_tokens.T, half_set, half_set.T, other_set, other_set.T,
            chip_grads, chip_grads.T,
            n1, n2, n3, n4)

        if nxy > 1:
            pieces = lax.all_to_all(part, "dp", 0, 0, axis_index_groups=plane_groups, tiled=True)
        else:
            pieces = part
        plane_sum = jnp.sum(pieces.astype(F32), axis=0).astype(BF)
        rows, cols = 64 // nx, 1024 // ny
        by_chip = plane_sum.reshape(4, 4, rows, cols)
        by_chip = lax.all_to_all(by_chip, "seq", 0, 0, axis_index_groups=quad_groups, tiled=True)
        quad_sum = jnp.sum(by_chip.astype(F32).reshape(2, 2, 4, rows, cols), axis=0).astype(BF)
        by_quad = quad_sum.transpose(1, 0, 2, 3)
        by_quad = lax.all_to_all(jnp.concatenate([by_quad] * nzh, axis=0), both, 0, 0,
                                 axis_index_groups=line_groups, tiled=True)
        line_sum = jnp.sum(by_quad.astype(F32), axis=0).astype(BF)
        spread = jnp.broadcast_to(line_sum[None], (nxy, 2, rows, cols))
        if nxy > 1:
            spread = lax.all_to_all(spread, "dp", 0, 0, axis_index_groups=plane_groups, tiled=True)
        slots = 4 // ny
        full = spread.reshape(nx, ny, 2, rows, slots, 256).transpose(0, 3, 1, 4, 2, 5).reshape(64, 4, 512)
        total = 128 * seq_count * dp_count
        grad_weights = full.astype(F32) * (1.0 / math.sqrt(total))

        layer_out = (layer_own + swap_core(layer_send).astype(F32)).astype(BF)

        b1 = lax.ppermute(grad_send, "seq", chip_swap(0))
        joined = grad_keep + b1[128:256].astype(F32)
        b2 = lax.ppermute(jnp.concatenate([joined[0:64], joined[96:128]], 0).astype(BF), "seq", chip_swap(1))
        b3 = lax.ppermute((joined[64:96] + b2[64:96].astype(F32)).astype(BF), "seq", chip_swap(2))
        returned = jnp.concatenate([b1[0:128], b2[0:64], b3], 0)
        dkv = (grad_own + nn(jnp.asarray(coarse_matrix.T, BF), returned)).astype(BF)
        back = jnp.concatenate([dquery, dkv], axis=1)
        partial = nt(back, weight[:, 0:768])
        mine = lax.dynamic_slice(partial, (core * 128, 0), (128, 1024))
        theirs = lax.dynamic_slice(partial, ((1 - core) * 128, 0), (128, 1024)).astype(BF)
        grad_tokens = (mine + swap_core(theirs).astype(F32)).astype(BF)
        return layer_out[None], grad_tokens[None], grad_weights

    return per_device


def solution(mesh):
    dp_count, seq_count = mesh.shape["dp"], mesh.shape["seq"]
    side = 4 if dp_count >= 16 else (2 if dp_count >= 4 else 1)
    specs = (P("dp", "seq", None), P("dp", "seq", None), P("seq", None, None))
    return jax.shard_map(
        make_device(side, side, dp_count, seq_count),
        mesh=mesh, in_specs=specs, out_specs=specs, check_vma=False)
```

```python
import functools
import math

import jax
import jax.numpy as jnp
import numpy as np
from jax import lax
from jax.experimental import pallas as pl
from jax.experimental.pallas import tpu as pltpu
from jax.sharding import PartitionSpec as P

HEAD = 64
LOG_TWO = math.log(2.0)
BF = jnp.bfloat16
F32 = jnp.float32

ROW_LEVELS = ((0, 256, 0), (256, 320, 2), (320, 384, 3), (384, 512, 1), (512, 576, 2), (576, 640, 3))


def nn(a, b):
    return lax.dot_general(a, b, (((1,), (0,)), ((), ())), preferred_element_type=F32)


def nt(a, b):
    return lax.dot_general(a, b, (((1,), (1,)), ((), ())), preferred_element_type=F32)


def layer_kernel(nx, ny, pos_ref, *refs):
    sources, refs = refs[:12], refs[12:]
    results, refs = refs[:8], refs[8:]
    staged, refs = refs[:8], refs[8:]
    (tok_s, tokt_s, g_s, gt_s, kv_s, kvt_s, qm_s, gm_s, gkv_s, attt_s, dqt_s, att_s, in_sem, w_sem, out_sem, part_sem) = refs
    own, ownt, mine, minet, other, othert, g, gt, n1, n2, n3, n4 = sources
    w_s, part_s, lown_s, lsend_s, dq_s, gown_s, gkeep_s, gsend_s = staged
    zl = pos_ref[0]
    core = pos_ref[1]
    even = lax.rem(zl + core, 2) == 0
    base = jnp.where(even, zl, zl + 7)
    turn = jnp.where(even, 2, -2)
    moves = []
    for piece, start in ((n1, base), (n2, base - turn), (n3, base + turn), (n4, base + 4)):
        for k in range(2):
            row = pl.multiple_of(lax.rem(start + k + 8, 8) * 128, 128)
            moves.append((piece.at[pl.ds(128 * k, 128), :], w_s.at[pl.ds(row, 128), :]))
    weight_copies = [pltpu.make_async_copy(src, dst, w_sem.at[i]) for i, (src, dst) in enumerate(moves)]
    here = pl.ds(pl.multiple_of(core * 512, 512), 512)
    there = pl.ds(pl.multiple_of((1 - core) * 512, 512), 512)
    pairs = (
        (own, tok_s.at[pl.ds(0, 256), :]),
        (mine, tok_s.at[pl.ds(256, 384), here]),
        (other, tok_s.at[pl.ds(256, 384), there]),
        (g, g_s),
        (ownt, tokt_s.at[:, pl.ds(0, 256)]),
        (minet, tokt_s.at[here, pl.ds(256, 384)]),
        (othert, tokt_s.at[there, pl.ds(256, 384)]),
        (gt, gt_s),
    )
    inputs = [pltpu.make_async_copy(src, dst, in_sem.at[i]) for i, (src, dst) in enumerate(pairs)]
    for copy in inputs[:3] + weight_copies + inputs[3:]:
        copy.start()
    outputs = {i: pltpu.make_async_copy(staged[i], results[i], out_sem.at[i]) for i in (0, 2, 3, 4, 5, 6, 7)}
    for copy in inputs[:3] + weight_copies:
        copy.wait()
    outputs[0].start()

    def project_keys(step, carry):
        row = pl.multiple_of(step * 128, 128)
        block = nn(tok_s[pl.ds(row, 128), :], w_s[:, 256:768])
        kv_s[pl.ds(row, 128), :] = block.astype(BF)
        kvt_s[:, pl.ds(row, 128)] = block.T.astype(BF)
        return carry

    lax.fori_loop(0, 5, project_keys, 0)
    queries = nn(tok_s[0:256, :], w_s[:, 0:256]) * 0.125
    inputs[3].wait()
    grads = nn(g_s[...], w_s[:, 768:1024])
    lane = lax.broadcasted_iota(jnp.int32, (256, 128), 1)
    for head in range(4):
        pair = (head // 2) * 128
        mine = (lane >= 64) if head % 2 else (lane < 64)
        qm_s[head] = jnp.where(mine, queries[:, pair:pair + 128], 0.0).astype(BF)
        gm_s[head] = jnp.where(mine, grads[:, pair:pair + 128], 0.0).astype(BF)

    for pair in range(2):
        kcol = pair * 128
        vcol = 256 + pair * 128
        key_grad = None
        value_grad = None
        for half in range(2):
            head = 2 * pair + half
            qm = qm_s[head]
            gm = gm_s[head]
            raw = nt(kv_s[:, kcol:kcol + 128], qm)
            scores = jnp.concatenate(
                [raw[lo:hi] + level * LOG_TWO if level else raw[lo:hi] for lo, hi, level in ROW_LEVELS], axis=0)
            exponent = jnp.exp(scores - jnp.max(scores, axis=0, keepdims=True))
            weights = exponent * (1.0 / jnp.sum(exponent, axis=0, keepdims=True))
            low = weights.astype(BF)
            dprobs = nt(kv_s[:, vcol:vcol + 128], gm)
            rowdot = jnp.sum(weights * dprobs, axis=0, keepdims=True)
            dscore = (weights * (dprobs - rowdot)).astype(BF)
            rows = slice(head * 64, head * 64 + 64)
            attt_s[rows, :] = nn(kvt_s[256 + head * 64:320 + head * 64, :], low)
            dqt_s[rows, :] = nn(kvt_s[rows, :], dscore) * 0.125
            new_key = nn(dscore, qm)
            new_value = nn(low, gm)
            key_grad = new_key if key_grad is None else key_grad + new_key
            value_grad = new_value if value_grad is None else value_grad + new_value
        for col, grad in ((kcol, key_grad), (vcol, value_grad)):
            where = slice(col, col + 128)
            gown_s[:, where] = grad[0:256]
            gkeep_s[:, where] = grad[256:384]
            gkv_s[:, where] = grad.astype(BF)

    gsend_s[...] = gkv_s[384:640, :]
    dq_s[...] = dqt_s[...].T.astype(BF)
    attended = attt_s[...].T.astype(BF)
    att_s[0] = attended[0:128]
    att_s[1] = attended[128:256]
    for index in (4, 5, 6, 7):
        outputs[index].start()

    x_rows = 64 // nx
    y_cols = 1024 // ny
    for copy in inputs[4:]:
        copy.wait()

    def part_copy(low):
        where = pl.ds(8 * low, 8)
        return pltpu.make_async_copy(part_s.at[:, where], results[1].at[:, where], part_sem.at[low])

    def grad_rows(low, quad, carry):
        rows = pl.ds(pl.multiple_of((2 * quad + low) * 128, 128), 128)
        lhs = tokt_s[rows, :]
        att_all = jnp.concatenate([att_s[0], att_s[1]], axis=0)
        block = jnp.concatenate(
            [nn(lhs[:, 0:256], dq_s[...]).astype(BF), nn(lhs, gkv_s[...]).astype(BF),
             nn(gt_s[rows, :], att_all).astype(BF)], axis=1)
        for side in range(2):
            for x in range(nx):
                for y in range(ny):
                    part_s[x * ny + y, (2 * low + side) * 4 + quad] = block[
                        side * 64 + x * x_rows:side * 64 + (x + 1) * x_rows, y * y_cols:(y + 1) * y_cols]
        return carry

    for low in range(2):
        lax.fori_loop(0, 4, functools.partial(grad_rows, low), 0)
        part_copy(low).start()
    lown_s[...] = nt(att_s[core], w_s[:, 768:1024])
    lsend_s[...] = nt(att_s[1 - core], w_s[:, 768:1024]).astype(BF)
    outputs[2].start()
    outputs[3].start()
    for low in range(2):
        part_copy(low).wait()
    for index in (0, 2, 3, 4, 5, 6, 7):
        outputs[index].wait()


def run_layer(nx, ny, *operands):
    anywhere = pl.BlockSpec(memory_space=pl.ANY)
    smem = pl.BlockSpec(memory_space=pltpu.SMEM)
    results = (
        ((1024, 1024), BF),
        ((nx * ny, 16, 64 // nx, 1024 // ny), BF),
        ((128, 1024), F32),
        ((128, 1024), BF),
        ((256, 256), BF),
        ((256, 512), F32),
        ((128, 512), F32),
        ((256, 512), BF),
    )
    return pl.pallas_call(
        functools.partial(layer_kernel, nx, ny),
        out_shape=tuple(jax.ShapeDtypeStruct(*result) for result in results),
        in_specs=[smem] + [anywhere] * (len(operands) - 1),
        out_specs=tuple([anywhere] * len(results)),
        scratch_shapes=[pltpu.VMEM(*result) for result in results] + [
            pltpu.VMEM((640, 1024), BF),
            pltpu.VMEM((1024, 640), BF),
            pltpu.VMEM((256, 1024), BF),
            pltpu.VMEM((1024, 256), BF),
            pltpu.VMEM((640, 512), BF),
            pltpu.VMEM((512, 640), BF),
            pltpu.VMEM((4, 256, 128), BF),
            pltpu.VMEM((4, 256, 128), BF),
            pltpu.VMEM((640, 512), BF),
            pltpu.VMEM((256, 256), F32),
            pltpu.VMEM((256, 256), F32),
            pltpu.VMEM((2, 128, 256), BF),
            pltpu.SemaphoreType.DMA((8,)),
            pltpu.SemaphoreType.DMA((8,)),
            pltpu.SemaphoreType.DMA((8,)),
            pltpu.SemaphoreType.DMA((2,)),
        ],
        compiler_params=pltpu.CompilerParams(vmem_limit_bytes=60 * 1024 * 1024),
        cost_estimate=pl.CostEstimate(flops=3_500_000_000, bytes_accessed=14_000_000, transcendentals=700_000),
    )(*operands)


def coarsening():
    matrix = np.zeros((224, 256), np.float32)
    base = 0
    for level in (1, 2, 3):
        for row in range(256 >> level):
            matrix[base + row, row << level:(row + 1) << level] = 0.5 ** level
        base += 256 >> level
    return matrix


def make_device(nx, ny, dp_count, seq_count):
    nxy = nx * ny
    nzh = dp_count // nxy
    ring = nzh * 8
    core_pairs = [(i, i ^ 1) for i in range(seq_count)]

    def chip_swap(bit):
        return [(i, i ^ (2 << bit)) for i in range(seq_count)]

    def device(z, xy, core):
        return ((z // 8) * nxy + xy) * seq_count + (z % 8) * 2 + core

    def swaps(turn):
        return [(device((z + 1 if (z + core + turn) % 2 == 0 else z - 1) % ring, xy, core), device(z, xy, core))
                for z in range(ring) for xy in range(nxy) for core in range(2)]

    swap_even, swap_odd = swaps(0), swaps(1)
    line_groups = [[(zh * nxy + xy) * seq_count + 4 * quad + i for zh in range(nzh) for i in range(4) for quad in range(4)]
                   for xy in range(nxy)]
    plane_groups = [[zh * nxy + xy for xy in range(nxy)] for zh in range(nzh)]
    coarse_matrix = coarsening()

    def swap_core(value):
        return lax.ppermute(value, "seq", core_pairs)

    def per_device(tokens, grad_out, stacked):
        seq = lax.axis_index("seq")
        zl = seq >> 1
        core = seq & 1
        first = core == 0

        def ordered(mine, other, axis):
            return jnp.where(first, jnp.concatenate([mine, other], axis), jnp.concatenate([other, mine], axis))

        both = ("dp", "seq")
        def shard_half(which):
            return lax.dynamic_slice(stacked, (0, 0, which * 256), (64, 4, 256)).reshape(64, 1024)

        keep, give = shard_half(core), shard_half(1 - core)
        shard_got = swap_core(give)
        w0 = ordered(keep, shard_got, 0)

        own = jnp.concatenate([tokens[0], grad_out[0]], axis=0)
        got = swap_core(own)
        chip_tokens = ordered(own[0:128], got[0:128], 0)
        chip_grads = ordered(own[128:256], got[128:256], 0)
        matrix = jnp.asarray(coarse_matrix, BF)
        half_tokens = lax.dynamic_slice(chip_tokens, (0, core * 512), (256, 512))
        coarse = nn(matrix, half_tokens).astype(BF)
        c1, c2, c3 = coarse[0:128], coarse[128:192], coarse[192:224]

        even = (zl + core) & 1 == 0
        w0, c3 = lax.optimization_barrier((w0, c3))
        t3 = lax.ppermute(c3, "seq", chip_swap(2))
        w1 = lax.ppermute(w0, both, swap_even)
        n1 = jnp.where(even, jnp.concatenate([w0, w1], 0), jnp.concatenate([w1, w0], 0))
        n1, to_second, t3 = lax.optimization_barrier((n1, jnp.concatenate([c2, t3], 0), t3))
        second = lax.ppermute(to_second, "seq", chip_swap(1))
        n2 = lax.ppermute(n1, both, swap_odd)
        held = jnp.concatenate([second[0:64], t3, second[64:96]], 0)
        n2, to_third, held = lax.optimization_barrier((n2, jnp.concatenate([c1, held], 0), held))
        third = lax.ppermute(to_third, "seq", chip_swap(0))
        n3 = lax.ppermute(n2, both, swap_even)
        n3, half_set = lax.optimization_barrier((n3, jnp.concatenate([held, third], 0)))
        n4 = lax.ppermute(n3, both, swap_odd)
        other_set = swap_core(half_set)

        position = jnp.stack([zl, core]).astype(jnp.int32)
        (weight, part, layer_own, layer_send, dquery, grad_own, grad_keep, grad_send) = run_layer(
            nx, ny, position, chip_tokens, chip_tokens.T, half_set, half_set.T, other_set, other_set.T,
            chip_grads, chip_grads.T,
            n1, n2, n3, n4)

        if nxy > 1:
            pieces = lax.all_to_all(part, "dp", 0, 0, axis_index_groups=plane_groups, tiled=True)
        else:
            pieces = part
        plane_sum = jnp.sum(pieces.astype(F32), axis=0).astype(BF)
        rows, cols = 64 // nx, 1024 // ny
        copies = jnp.broadcast_to(plane_sum[None], (nzh, 16, rows, cols)).reshape(nzh * 16, rows, cols)
        columns = lax.all_to_all(copies, both, 0, 0, axis_index_groups=line_groups, tiled=True)
        line_sum = jnp.sum(columns.astype(F32).reshape(nzh * 2, 2, 4, rows, cols), axis=(0, 2)).astype(BF)
        spread = jnp.broadcast_to(line_sum[None], (nxy, 2, rows, cols))
        if nxy > 1:
            spread = lax.all_to_all(spread, "dp", 0, 0, axis_index_groups=plane_groups, tiled=True)
        slots = 4 // ny
        full = spread.reshape(nx, ny, 2, rows, slots, 256).transpose(0, 3, 1, 4, 2, 5).reshape(64, 4, 512)
        total = 128 * seq_count * dp_count
        grad_weights = full.astype(F32) * (1.0 / math.sqrt(total))

        layer_out = (layer_own + swap_core(layer_send).astype(F32)).astype(BF)

        b1 = lax.ppermute(grad_send, "seq", chip_swap(0))
        joined = grad_keep + b1[128:256].astype(F32)
        b2 = lax.ppermute(jnp.concatenate([joined[0:64], joined[96:128]], 0).astype(BF), "seq", chip_swap(1))
        b3 = lax.ppermute((joined[64:96] + b2[64:96].astype(F32)).astype(BF), "seq", chip_swap(2))
        returned = jnp.concatenate([b1[0:128], b2[0:64], b3], 0)
        dkv = (grad_own + nn(jnp.asarray(coarse_matrix.T, BF), returned)).astype(BF)
        back = jnp.concatenate([dquery, dkv], axis=1)
        partial = nt(back, weight[:, 0:768])
        mine = lax.dynamic_slice(partial, (core * 128, 0), (128, 1024))
        theirs = lax.dynamic_slice(partial, ((1 - core) * 128, 0), (128, 1024)).astype(BF)
        grad_tokens = (mine + swap_core(theirs).astype(F32)).astype(BF)
        return layer_out[None], grad_tokens[None], grad_weights

    return per_device


def solution(mesh):
    dp_count, seq_count = mesh.shape["dp"], mesh.shape["seq"]
    side = 4 if dp_count >= 16 else (2 if dp_count >= 4 else 1)
    specs = (P("dp", "seq", None), P("dp", "seq", None), P("seq", None, None))
    return jax.shard_map(
        make_device(side, side, dp_count, seq_count),
        mesh=mesh, in_specs=specs, out_specs=specs, check_vma=False)
```

```python
import functools
import math

import jax
import jax.numpy as jnp
import numpy as np
from jax import lax
from jax.experimental import pallas as pl
from jax.experimental.pallas import tpu as pltpu
from jax.sharding import PartitionSpec as P

HEAD = 64
LOG_TWO = math.log(2.0)
BF = jnp.bfloat16
F32 = jnp.float32

ROW_LEVELS = ((0, 256, 0), (256, 320, 2), (320, 384, 3), (384, 512, 1), (512, 576, 2), (576, 640, 3))


def nn(a, b):
    return lax.dot_general(a, b, (((1,), (0,)), ((), ())), preferred_element_type=F32)


def nt(a, b):
    return lax.dot_general(a, b, (((1,), (1,)), ((), ())), preferred_element_type=F32)


def layer_kernel(nx, ny, pos_ref, *refs):
    sources, refs = refs[:12], refs[12:]
    results, refs = refs[:9], refs[9:]
    staged, refs = refs[:9], refs[9:]
    (tok_s, tokt_s, g_s, gt_s, kv_s, kvt_s, qm_s, gm_s, gkv_s, attt_s, dqt_s, att_s, in_sem, w_sem, out_sem, part_sem) = refs
    own, ownt, mine, minet, other, othert, g, gt, n1, n2, n3, n4 = sources
    w_s, lown_s, lsend_s, dq_s, gown_s, gkeep_s, gsend_s = staged[:1] + staged[3:]
    part_s, part_out = staged[1:3], results[1:3]
    zl = pos_ref[0]
    core = pos_ref[1]
    even = lax.rem(zl + core, 2) == 0
    base = jnp.where(even, zl, zl + 7)
    turn = jnp.where(even, 2, -2)
    moves = []
    for piece, start in ((n1, base), (n2, base - turn), (n3, base + turn), (n4, base + 4)):
        for k in range(2):
            row = pl.multiple_of(lax.rem(start + k + 8, 8) * 128, 128)
            moves.append((piece.at[pl.ds(128 * k, 128), :], w_s.at[pl.ds(row, 128), :]))
    weight_copies = [pltpu.make_async_copy(src, dst, w_sem.at[i]) for i, (src, dst) in enumerate(moves)]
    here = pl.ds(pl.multiple_of(core * 512, 512), 512)
    there = pl.ds(pl.multiple_of((1 - core) * 512, 512), 512)
    pairs = (
        (own, tok_s.at[pl.ds(0, 256), :]),
        (mine, tok_s.at[pl.ds(256, 384), here]),
        (other, tok_s.at[pl.ds(256, 384), there]),
        (g, g_s),
        (ownt, tokt_s.at[:, pl.ds(0, 256)]),
        (minet, tokt_s.at[here, pl.ds(256, 384)]),
        (othert, tokt_s.at[there, pl.ds(256, 384)]),
        (gt, gt_s),
    )
    inputs = [pltpu.make_async_copy(src, dst, in_sem.at[i]) for i, (src, dst) in enumerate(pairs)]
    for copy in inputs[:3] + weight_copies + inputs[3:]:
        copy.start()
    outputs = {i: pltpu.make_async_copy(staged[i], results[i], out_sem.at[i]) for i in (0, 3, 4, 5, 6, 7, 8)}
    for copy in inputs[:3] + weight_copies:
        copy.wait()
    outputs[0].start()

    def project_keys(step, carry):
        row = pl.multiple_of(step * 128, 128)
        block = nn(tok_s[pl.ds(row, 128), :], w_s[:, 256:768])
        kv_s[pl.ds(row, 128), :] = block.astype(BF)
        kvt_s[:, pl.ds(row, 128)] = block.T.astype(BF)
        return carry

    lax.fori_loop(0, 5, project_keys, 0)
    queries = nn(tok_s[0:256, :], w_s[:, 0:256]) * 0.125
    inputs[3].wait()
    grads = nn(g_s[...], w_s[:, 768:1024])
    lane = lax.broadcasted_iota(jnp.int32, (256, 128), 1)
    for head in range(4):
        pair = (head // 2) * 128
        mine = (lane >= 64) if head % 2 else (lane < 64)
        qm_s[head] = jnp.where(mine, queries[:, pair:pair + 128], 0.0).astype(BF)
        gm_s[head] = jnp.where(mine, grads[:, pair:pair + 128], 0.0).astype(BF)

    for pair in range(2):
        kcol = pair * 128
        vcol = 256 + pair * 128
        key_grad = None
        value_grad = None
        for half in range(2):
            head = 2 * pair + half
            qm = qm_s[head]
            gm = gm_s[head]
            raw = nt(kv_s[:, kcol:kcol + 128], qm)
            scores = jnp.concatenate(
                [raw[lo:hi] + level * LOG_TWO if level else raw[lo:hi] for lo, hi, level in ROW_LEVELS], axis=0)
            exponent = jnp.exp(scores - jnp.max(scores, axis=0, keepdims=True))
            weights = exponent * (1.0 / jnp.sum(exponent, axis=0, keepdims=True))
            low = weights.astype(BF)
            dprobs = nt(kv_s[:, vcol:vcol + 128], gm)
            rowdot = jnp.sum(weights * dprobs, axis=0, keepdims=True)
            dscore = (weights * (dprobs - rowdot)).astype(BF)
            rows = slice(head * 64, head * 64 + 64)
            attt_s[rows, :] = nn(kvt_s[256 + head * 64:320 + head * 64, :], low)
            dqt_s[rows, :] = nn(kvt_s[rows, :], dscore) * 0.125
            new_key = nn(dscore, qm)
            new_value = nn(low, gm)
            key_grad = new_key if key_grad is None else key_grad + new_key
            value_grad = new_value if value_grad is None else value_grad + new_value
        for col, grad in ((kcol, key_grad), (vcol, value_grad)):
            where = slice(col, col + 128)
            gown_s[:, where] = grad[0:256]
            gkeep_s[:, where] = grad[256:384]
            gkv_s[:, where] = grad.astype(BF)

    gsend_s[...] = gkv_s[384:640, :]
    dq_s[...] = dqt_s[...].T.astype(BF)
    attended = attt_s[...].T.astype(BF)
    att_s[0] = attended[0:128]
    att_s[1] = attended[128:256]
    for index in (5, 6, 7, 8):
        outputs[index].start()

    x_rows = 64 // nx
    y_cols = 512 // ny
    for copy in inputs[4:]:
        copy.wait()

    def part_copies(low):
        where = pl.ds(8 * low, 8)
        return [pltpu.make_async_copy(part_s[half].at[:, where], part_out[half].at[:, where], part_sem.at[low, half])
                for half in range(2)]

    def grad_rows(low, quad, carry):
        rows = pl.ds(pl.multiple_of((2 * quad + low) * 128, 128), 128)
        lhs = tokt_s[rows, :]
        att_all = jnp.concatenate([att_s[0], att_s[1]], axis=0)
        block = jnp.concatenate(
            [nn(lhs[:, 0:256], dq_s[...]).astype(BF), nn(lhs, gkv_s[...]).astype(BF),
             nn(gt_s[rows, :], att_all).astype(BF)], axis=1)
        for side in range(2):
            for x in range(nx):
                for y in range(ny):
                    for half in range(2):
                        col = (2 * y + half) * y_cols
                        part_s[half][x * ny + y, (2 * low + side) * 4 + quad] = block[
                            side * 64 + x * x_rows:side * 64 + (x + 1) * x_rows, col:col + y_cols]
        return carry

    for low in range(2):
        lax.fori_loop(0, 4, functools.partial(grad_rows, low), 0)
        for copy in part_copies(low):
            copy.start()
    lown_s[...] = nt(att_s[core], w_s[:, 768:1024])
    lsend_s[...] = nt(att_s[1 - core], w_s[:, 768:1024]).astype(BF)
    outputs[3].start()
    outputs[4].start()
    for low in range(2):
        for copy in part_copies(low):
            copy.wait()
    for index in (0, 3, 4, 5, 6, 7, 8):
        outputs[index].wait()


def run_layer(nx, ny, *operands):
    anywhere = pl.BlockSpec(memory_space=pl.ANY)
    smem = pl.BlockSpec(memory_space=pltpu.SMEM)
    results = (
        ((1024, 1024), BF),
        ((nx * ny, 16, 64 // nx, 512 // ny), BF),
        ((nx * ny, 16, 64 // nx, 512 // ny), BF),
        ((128, 1024), F32),
        ((128, 1024), BF),
        ((256, 256), BF),
        ((256, 512), F32),
        ((128, 512), F32),
        ((256, 512), BF),
    )
    return pl.pallas_call(
        functools.partial(layer_kernel, nx, ny),
        out_shape=tuple(jax.ShapeDtypeStruct(*result) for result in results),
        in_specs=[smem] + [anywhere] * (len(operands) - 1),
        out_specs=tuple([anywhere] * len(results)),
        scratch_shapes=[pltpu.VMEM(*result) for result in results] + [
            pltpu.VMEM((640, 1024), BF),
            pltpu.VMEM((1024, 640), BF),
            pltpu.VMEM((256, 1024), BF),
            pltpu.VMEM((1024, 256), BF),
            pltpu.VMEM((640, 512), BF),
            pltpu.VMEM((512, 640), BF),
            pltpu.VMEM((4, 256, 128), BF),
            pltpu.VMEM((4, 256, 128), BF),
            pltpu.VMEM((640, 512), BF),
            pltpu.VMEM((256, 256), F32),
            pltpu.VMEM((256, 256), F32),
            pltpu.VMEM((2, 128, 256), BF),
            pltpu.SemaphoreType.DMA((8,)),
            pltpu.SemaphoreType.DMA((8,)),
            pltpu.SemaphoreType.DMA((9,)),
            pltpu.SemaphoreType.DMA((2, 2)),
        ],
        compiler_params=pltpu.CompilerParams(vmem_limit_bytes=60 * 1024 * 1024),
        cost_estimate=pl.CostEstimate(flops=3_500_000_000, bytes_accessed=14_000_000, transcendentals=700_000),
    )(*operands)


def coarsening():
    matrix = np.zeros((224, 256), np.float32)
    base = 0
    for level in (1, 2, 3):
        for row in range(256 >> level):
            matrix[base + row, row << level:(row + 1) << level] = 0.5 ** level
        base += 256 >> level
    return matrix


def make_device(nx, ny, dp_count, seq_count):
    nxy = nx * ny
    nzh = dp_count // nxy
    ring = nzh * 8
    core_pairs = [(i, i ^ 1) for i in range(seq_count)]

    def chip_swap(bit):
        return [(i, i ^ (2 << bit)) for i in range(seq_count)]

    def device(z, xy, core):
        return ((z // 8) * nxy + xy) * seq_count + (z % 8) * 2 + core

    def swaps(turn):
        return [(device((z + 1 if (z + core + turn) % 2 == 0 else z - 1) % ring, xy, core), device(z, xy, core))
                for z in range(ring) for xy in range(nxy) for core in range(2)]

    swap_even, swap_odd = swaps(0), swaps(1)
    line_groups = [[(zh * nxy + xy) * seq_count + 4 * quad + i for zh in range(nzh) for i in range(4) for quad in range(4)]
                   for xy in range(nxy)]
    plane_groups = [[zh * nxy + xy for xy in range(nxy)] for zh in range(nzh)]
    coarse_matrix = coarsening()

    def swap_core(value):
        return lax.ppermute(value, "seq", core_pairs)

    def per_device(tokens, grad_out, stacked):
        seq = lax.axis_index("seq")
        zl = seq >> 1
        core = seq & 1
        first = core == 0

        def ordered(mine, other, axis):
            return jnp.where(first, jnp.concatenate([mine, other], axis), jnp.concatenate([other, mine], axis))

        both = ("dp", "seq")
        def shard_half(which):
            return lax.dynamic_slice(stacked, (0, 0, which * 256), (64, 4, 256)).reshape(64, 1024)

        keep, give = shard_half(core), shard_half(1 - core)
        shard_got = swap_core(give)
        w0 = ordered(keep, shard_got, 0)

        own = jnp.concatenate([tokens[0], grad_out[0]], axis=0)
        got = swap_core(own)
        chip_tokens = ordered(own[0:128], got[0:128], 0)
        chip_grads = ordered(own[128:256], got[128:256], 0)
        matrix = jnp.asarray(coarse_matrix, BF)
        half_tokens = lax.dynamic_slice(chip_tokens, (0, core * 512), (256, 512))
        coarse = nn(matrix, half_tokens).astype(BF)
        c1, c2, c3 = coarse[0:128], coarse[128:192], coarse[192:224]

        even = (zl + core) & 1 == 0
        w0, c3 = lax.optimization_barrier((w0, c3))
        t3 = lax.ppermute(c3, "seq", chip_swap(2))
        w1 = lax.ppermute(w0, both, swap_even)
        n1 = jnp.where(even, jnp.concatenate([w0, w1], 0), jnp.concatenate([w1, w0], 0))
        n1, to_second, t3 = lax.optimization_barrier((n1, jnp.concatenate([c2, t3], 0), t3))
        second = lax.ppermute(to_second, "seq", chip_swap(1))
        n2 = lax.ppermute(n1, both, swap_odd)
        held = jnp.concatenate([second[0:64], t3, second[64:96]], 0)
        n2, to_third, held = lax.optimization_barrier((n2, jnp.concatenate([c1, held], 0), held))
        third = lax.ppermute(to_third, "seq", chip_swap(0))
        n3 = lax.ppermute(n2, both, swap_even)
        n3, half_set = lax.optimization_barrier((n3, jnp.concatenate([held, third], 0)))
        n4 = lax.ppermute(n3, both, swap_odd)
        other_set = swap_core(half_set)

        position = jnp.stack([zl, core]).astype(jnp.int32)
        (weight, part_a, part_b, layer_own, layer_send, dquery, grad_own, grad_keep, grad_send) = run_layer(
            nx, ny, position, chip_tokens, chip_tokens.T, half_set, half_set.T, other_set, other_set.T,
            chip_grads, chip_grads.T,
            n1, n2, n3, n4)

        rows, cols = 64 // nx, 1024 // ny

        def reduced(part):
            if nxy > 1:
                part = lax.all_to_all(part, "dp", 0, 0, axis_index_groups=plane_groups, tiled=True)
            plane_sum = jnp.sum(part.astype(F32), axis=0).astype(BF)
            copies = jnp.broadcast_to(plane_sum[None], (nzh,) + plane_sum.shape).reshape(nzh * 16, rows, cols // 2)
            columns = lax.all_to_all(copies, both, 0, 0, axis_index_groups=line_groups, tiled=True)
            return jnp.sum(columns.astype(F32).reshape(nzh * 2, 2, 4, rows, cols // 2), axis=(0, 2)).astype(BF)

        line_sum = jnp.concatenate([reduced(part_a), reduced(part_b)], axis=-1)
        spread = jnp.broadcast_to(line_sum[None], (nxy, 2, rows, cols))
        if nxy > 1:
            spread = lax.all_to_all(spread, "dp", 0, 0, axis_index_groups=plane_groups, tiled=True)
        slots = 4 // ny
        full = spread.reshape(nx, ny, 2, rows, slots, 256).transpose(0, 3, 1, 4, 2, 5).reshape(64, 4, 512)
        total = 128 * seq_count * dp_count
        grad_weights = full.astype(F32) * (1.0 / math.sqrt(total))

        layer_out = (layer_own + swap_core(layer_send).astype(F32)).astype(BF)

        b1 = lax.ppermute(grad_send, "seq", chip_swap(0))
        joined = grad_keep + b1[128:256].astype(F32)
        b2 = lax.ppermute(jnp.concatenate([joined[0:64], joined[96:128]], 0).astype(BF), "seq", chip_swap(1))
        b3 = lax.ppermute((joined[64:96] + b2[64:96].astype(F32)).astype(BF), "seq", chip_swap(2))
        returned = jnp.concatenate([b1[0:128], b2[0:64], b3], 0)
        dkv = (grad_own + nn(jnp.asarray(coarse_matrix.T, BF), returned)).astype(BF)
        back = jnp.concatenate([dquery, dkv], axis=1)
        partial = nt(back, weight[:, 0:768])
        mine = lax.dynamic_slice(partial, (core * 128, 0), (128, 1024))
        theirs = lax.dynamic_slice(partial, ((1 - core) * 128, 0), (128, 1024)).astype(BF)
        grad_tokens = (mine + swap_core(theirs).astype(F32)).astype(BF)
        return layer_out[None], grad_tokens[None], grad_weights

    return per_device


def solution(mesh):
    dp_count, seq_count = mesh.shape["dp"], mesh.shape["seq"]
    side = 4 if dp_count >= 16 else (2 if dp_count >= 4 else 1)
    specs = (P("dp", "seq", None), P("dp", "seq", None), P("seq", None, None))
    return jax.shard_map(
        make_device(side, side, dp_count, seq_count),
        mesh=mesh, in_specs=specs, out_specs=specs, check_vma=False)
```

```python
import functools
import math

import jax
import jax.numpy as jnp
import numpy as np
from jax import lax
from jax.experimental import pallas as pl
from jax.experimental.pallas import tpu as pltpu
from jax.sharding import PartitionSpec as P

HEAD = 64
LOG_TWO = math.log(2.0)
BF = jnp.bfloat16
F32 = jnp.float32

ROW_LEVELS = ((0, 256, 0), (256, 288, 2), (288, 320, 3), (320, 384, 1), (384, 416, 2), (416, 448, 3),
              (448, 480, 2), (480, 512, 3), (512, 576, 1), (576, 608, 2), (608, 640, 3))
KEPT = ((0, 32, 0), (32, 16, 64), (48, 16, 96))
SENT = ((64, 64, 0), (128, 32, 128), (160, 16, 192), (176, 16, 224))

def nn(a, b):
    return lax.dot_general(a, b, (((1,), (0,)), ((), ())), preferred_element_type=F32)


def nt(a, b):
    return lax.dot_general(a, b, (((1,), (1,)), ((), ())), preferred_element_type=F32)


def layer_kernel(nx, ny, pos_ref, *refs):
    sources, refs = refs[:10], refs[10:]
    results, refs = refs[:8], refs[8:]
    staged, refs = refs[:8], refs[8:]
    (tok_s, tokt_s, g_s, gt_s, kv_s, kvt_s, qm_s, gm_s, gkv_s, attt_s, dqt_s, att_s, in_sem, w_sem, out_sem, part_sem) = refs
    own, ownt, rest, restt, g, gt, n1, n2, n3, n4 = sources
    w_s, part_s, lown_s, lsend_s, dq_s, gown_s, gkeep_s, gsend_s = staged
    zl = pos_ref[0]
    core = pos_ref[1]
    even = lax.rem(zl + core, 2) == 0
    base = jnp.where(even, zl, zl + 7)
    turn = jnp.where(even, 2, -2)
    moves = []
    for piece, start in ((n1, base), (n2, base - turn), (n3, base + turn), (n4, base + 4)):
        for k in range(2):
            row = pl.multiple_of(lax.rem(start + k + 8, 8) * 128, 128)
            moves.append((piece.at[pl.ds(128 * k, 128), :], w_s.at[pl.ds(row, 128), :]))
    weight_copies = [pltpu.make_async_copy(src, dst, w_sem.at[i]) for i, (src, dst) in enumerate(moves)]
    pairs = (
        (own, tok_s.at[pl.ds(0, 256), :]),
        (rest, tok_s.at[pl.ds(256, 384), :]),
        (g, g_s),
        (ownt, tokt_s.at[:, pl.ds(0, 256)]),
        (restt, tokt_s.at[:, pl.ds(256, 384)]),
        (gt, gt_s),
    )
    inputs = [pltpu.make_async_copy(src, dst, in_sem.at[i]) for i, (src, dst) in enumerate(pairs)]
    for copy in inputs[:2] + weight_copies + inputs[2:]:
        copy.start()
    outputs = {i: pltpu.make_async_copy(staged[i], results[i], out_sem.at[i]) for i in (0, 2, 3, 4, 5, 6, 7)}
    for copy in inputs[:2] + weight_copies:
        copy.wait()
    outputs[0].start()

    def project_keys(step, carry):
        row = pl.multiple_of(step * 128, 128)
        block = nn(tok_s[pl.ds(row, 128), :], w_s[:, 256:768])
        kv_s[pl.ds(row, 128), :] = block.astype(BF)
        kvt_s[:, pl.ds(row, 128)] = block.T.astype(BF)
        return carry

    lax.fori_loop(0, 5, project_keys, 0)
    queries = nn(tok_s[0:256, :], w_s[:, 0:256]) * 0.125
    inputs[2].wait()
    grads = nn(g_s[...], w_s[:, 768:1024])
    lane = lax.broadcasted_iota(jnp.int32, (256, 128), 1)
    for head in range(4):
        pair = (head // 2) * 128
        mine = (lane >= 64) if head % 2 else (lane < 64)
        qm_s[head] = jnp.where(mine, queries[:, pair:pair + 128], 0.0).astype(BF)
        gm_s[head] = jnp.where(mine, grads[:, pair:pair + 128], 0.0).astype(BF)

    for pair in range(2):
        kcol = pair * 128
        vcol = 256 + pair * 128
        key_grad = None
        value_grad = None
        for half in range(2):
            head = 2 * pair + half
            qm = qm_s[head]
            gm = gm_s[head]
            raw = nt(kv_s[:, kcol:kcol + 128], qm)
            scores = jnp.concatenate(
                [raw[lo:hi] + level * LOG_TWO if level else raw[lo:hi] for lo, hi, level in ROW_LEVELS], axis=0)
            exponent = jnp.exp(scores - jnp.max(scores, axis=0, keepdims=True))
            weights = exponent * (1.0 / jnp.sum(exponent, axis=0, keepdims=True))
            low = weights.astype(BF)
            dprobs = nt(kv_s[:, vcol:vcol + 128], gm)
            rowdot = jnp.sum(weights * dprobs, axis=0, keepdims=True)
            dscore = (weights * (dprobs - rowdot)).astype(BF)
            rows = slice(head * 64, head * 64 + 64)
            attt_s[rows, :] = nn(kvt_s[256 + head * 64:320 + head * 64, :], low)
            dqt_s[rows, :] = nn(kvt_s[rows, :], dscore) * 0.125
            new_key = nn(dscore, qm)
            new_value = nn(low, gm)
            key_grad = new_key if key_grad is None else key_grad + new_key
            value_grad = new_value if value_grad is None else value_grad + new_value
        for col, grad in ((kcol, key_grad), (vcol, value_grad)):
            where = slice(col, col + 128)
            gown_s[:, where] = grad[0:256]
            for part in range(2):
                for start, count, to in KEPT:
                    first = 256 + 192 * part + start
                    gkeep_s[to + count * part:to + count * part + count, where] = grad[first:first + count]
            gkv_s[:, where] = grad.astype(BF)

    for part in range(2):
        for start, count, to in SENT:
            first = 256 + 192 * part + start
            gsend_s[to + count * part:to + count * part + count, :] = gkv_s[first:first + count, :]
    dq_s[...] = dqt_s[...].T.astype(BF)
    attended = attt_s[...].T.astype(BF)
    att_s[0] = attended[0:128]
    att_s[1] = attended[128:256]
    for index in (4, 5, 6, 7):
        outputs[index].start()

    x_rows = 64 // nx
    y_cols = 1024 // ny
    for copy in inputs[3:]:
        copy.wait()

    def part_copy(low):
        where = pl.ds(8 * low, 8)
        return pltpu.make_async_copy(part_s.at[:, where], results[1].at[:, where], part_sem.at[low])

    def grad_rows(low, quad, carry):
        rows = pl.ds(pl.multiple_of((2 * quad + low) * 128, 128), 128)
        lhs = tokt_s[rows, :]
        att_all = jnp.concatenate([att_s[0], att_s[1]], axis=0)
        block = jnp.concatenate(
            [nn(lhs[:, 0:256], dq_s[...]).astype(BF), nn(lhs, gkv_s[...]).astype(BF),
             nn(gt_s[rows, :], att_all).astype(BF)], axis=1)
        for side in range(2):
            for x in range(nx):
                for y in range(ny):
                    part_s[x * ny + y, (2 * low + side) * 4 + quad] = block[
                        side * 64 + x * x_rows:side * 64 + (x + 1) * x_rows, y * y_cols:(y + 1) * y_cols]
        return carry

    for low in range(2):
        lax.fori_loop(0, 4, functools.partial(grad_rows, low), 0)
        part_copy(low).start()
    lown_s[...] = nt(att_s[core], w_s[:, 768:1024])
    lsend_s[...] = nt(att_s[1 - core], w_s[:, 768:1024]).astype(BF)
    outputs[2].start()
    outputs[3].start()
    for low in range(2):
        part_copy(low).wait()
    for index in (0, 2, 3, 4, 5, 6, 7):
        outputs[index].wait()


def run_layer(nx, ny, *operands):
    anywhere = pl.BlockSpec(memory_space=pl.ANY)
    smem = pl.BlockSpec(memory_space=pltpu.SMEM)
    results = (
        ((1024, 1024), BF),
        ((nx * ny, 16, 64 // nx, 1024 // ny), BF),
        ((128, 1024), F32),
        ((128, 1024), BF),
        ((256, 256), BF),
        ((256, 512), F32),
        ((128, 512), F32),
        ((256, 512), BF),
    )
    return pl.pallas_call(
        functools.partial(layer_kernel, nx, ny),
        out_shape=tuple(jax.ShapeDtypeStruct(*result) for result in results),
        in_specs=[smem] + [anywhere] * (len(operands) - 1),
        out_specs=tuple([anywhere] * len(results)),
        scratch_shapes=[pltpu.VMEM(*result) for result in results] + [
            pltpu.VMEM((640, 1024), BF),
            pltpu.VMEM((1024, 640), BF),
            pltpu.VMEM((256, 1024), BF),
            pltpu.VMEM((1024, 256), BF),
            pltpu.VMEM((640, 512), BF),
            pltpu.VMEM((512, 640), BF),
            pltpu.VMEM((4, 256, 128), BF),
            pltpu.VMEM((4, 256, 128), BF),
            pltpu.VMEM((640, 512), BF),
            pltpu.VMEM((256, 256), F32),
            pltpu.VMEM((256, 256), F32),
            pltpu.VMEM((2, 128, 256), BF),
            pltpu.SemaphoreType.DMA((8,)),
            pltpu.SemaphoreType.DMA((8,)),
            pltpu.SemaphoreType.DMA((8,)),
            pltpu.SemaphoreType.DMA((2,)),
        ],
        compiler_params=pltpu.CompilerParams(vmem_limit_bytes=60 * 1024 * 1024),
        cost_estimate=pl.CostEstimate(flops=3_500_000_000, bytes_accessed=14_000_000, transcendentals=700_000),
    )(*operands)


def coarsening(count):
    matrix = np.zeros((count * 7 // 8, count), np.float32)
    base = 0
    for level in (1, 2, 3):
        for row in range(count >> level):
            matrix[base + row, row << level:(row + 1) << level] = 0.5 ** level
        base += count >> level
    return matrix


def make_device(nx, ny, dp_count, seq_count):
    nxy = nx * ny
    nzh = dp_count // nxy
    ring = nzh * 8
    core_pairs = [(i, i ^ 1) for i in range(seq_count)]

    def chip_swap(bit):
        return [(i, i ^ (2 << bit)) for i in range(seq_count)]

    def device(z, xy, core):
        return ((z // 8) * nxy + xy) * seq_count + (z % 8) * 2 + core

    def swaps(turn):
        return [(device((z + 1 if (z + core + turn) % 2 == 0 else z - 1) % ring, xy, core), device(z, xy, core))
                for z in range(ring) for xy in range(nxy) for core in range(2)]

    swap_even, swap_odd = swaps(0), swaps(1)
    line_groups = [[(zh * nxy + xy) * seq_count + 4 * quad + i for zh in range(nzh) for i in range(4) for quad in range(4)]
                   for xy in range(nxy)]
    plane_groups = [[zh * nxy + xy for xy in range(nxy)] for zh in range(nzh)]
    coarse_matrix = coarsening(256)

    def swap_core(value):
        return lax.ppermute(value, "seq", core_pairs)

    def per_device(tokens, grad_out, stacked):
        seq = lax.axis_index("seq")
        zl = seq >> 1
        core = seq & 1
        first = core == 0

        def ordered(mine, other, axis):
            return jnp.where(first, jnp.concatenate([mine, other], axis), jnp.concatenate([other, mine], axis))

        both = ("dp", "seq")
        def shard_half(which):
            return lax.dynamic_slice(stacked, (0, 0, which * 256), (64, 4, 256)).reshape(64, 1024)

        keep, give = shard_half(core), shard_half(1 - core)
        shard_got = swap_core(give)
        w0 = ordered(keep, shard_got, 0)

        own = jnp.concatenate([tokens[0], grad_out[0]], axis=0)
        got = swap_core(own)
        chip_tokens = ordered(own[0:128], got[0:128], 0)
        chip_grads = ordered(own[128:256], got[128:256], 0)
        coarse = nn(jnp.asarray(coarsening(128), BF), tokens[0]).astype(BF)
        c1, c2, c3 = coarse[0:64], coarse[64:96], coarse[96:112]

        even = (zl + core) & 1 == 0
        t3 = lax.ppermute(c3, "seq", chip_swap(2))
        w0, to_second, t3 = lax.optimization_barrier((w0, jnp.concatenate([c2, t3], 0), t3))
        second = lax.ppermute(to_second, "seq", chip_swap(1))
        w1 = lax.ppermute(w0, both, swap_even)
        held = jnp.concatenate([second[0:32], t3, second[32:48]], 0)
        w1, to_third, held = lax.optimization_barrier((w1, jnp.concatenate([c1, held], 0), held))
        third = lax.ppermute(to_third, "seq", chip_swap(0))
        n1 = jnp.where(even, jnp.concatenate([w0, w1], 0), jnp.concatenate([w1, w0], 0))
        n2 = lax.ppermute(n1, both, swap_odd)
        n2, half_set = lax.optimization_barrier((n2, jnp.concatenate([held, third], 0)))
        other_set = swap_core(half_set)
        n3 = lax.ppermute(n2, both, swap_even)
        n3, rest, chip_tokens, chip_grads = lax.optimization_barrier(
            (n3, ordered(half_set, other_set, 0), chip_tokens, chip_grads))
        n4 = lax.ppermute(n3, both, swap_odd)

        position = jnp.stack([zl, core]).astype(jnp.int32)
        (weight, part, layer_own, layer_send, dquery, grad_own, grad_keep, grad_send) = run_layer(
            nx, ny, position, chip_tokens, chip_tokens.T, rest, rest.T,
            chip_grads, chip_grads.T,
            n1, n2, n3, n4)

        if nxy > 1:
            pieces = lax.all_to_all(part, "dp", 0, 0, axis_index_groups=plane_groups, tiled=True)
        else:
            pieces = part
        plane_sum = jnp.sum(pieces.astype(F32), axis=0).astype(BF)
        rows, cols = 64 // nx, 1024 // ny
        copies = jnp.broadcast_to(plane_sum[None], (nzh, 16, rows, cols)).reshape(nzh * 16, rows, cols)
        columns = lax.all_to_all(copies, both, 0, 0, axis_index_groups=line_groups, tiled=True)
        line_sum = jnp.sum(columns.astype(F32).reshape(nzh * 2, 2, 4, rows, cols), axis=(0, 2)).astype(BF)
        spread = jnp.broadcast_to(line_sum[None], (nxy, 2, rows, cols))
        if nxy > 1:
            spread = lax.all_to_all(spread, "dp", 0, 0, axis_index_groups=plane_groups, tiled=True)
        slots = 4 // ny
        full = spread.reshape(nx, ny, 2, rows, slots, 256).transpose(0, 3, 1, 4, 2, 5).reshape(64, 4, 512)
        total = 128 * seq_count * dp_count
        grad_weights = full.astype(F32) * (1.0 / math.sqrt(total))

        layer_out = (layer_own + swap_core(layer_send).astype(F32)).astype(BF)

        b1 = lax.ppermute(grad_send, "seq", chip_swap(0))
        joined = grad_keep + b1[128:256].astype(F32)
        b2 = lax.ppermute(jnp.concatenate([joined[0:64], joined[96:128]], 0).astype(BF), "seq", chip_swap(1))
        b3 = lax.ppermute((joined[64:96] + b2[64:96].astype(F32)).astype(BF), "seq", chip_swap(2))
        returned = jnp.concatenate([b1[0:128], b2[0:64], b3], 0)
        dkv = (grad_own + nn(jnp.asarray(coarse_matrix.T, BF), returned)).astype(BF)
        back = jnp.concatenate([dquery, dkv], axis=1)
        partial = nt(back, weight[:, 0:768])
        mine = lax.dynamic_slice(partial, (core * 128, 0), (128, 1024))
        theirs = lax.dynamic_slice(partial, ((1 - core) * 128, 0), (128, 1024)).astype(BF)
        grad_tokens = (mine + swap_core(theirs).astype(F32)).astype(BF)
        return layer_out[None], grad_tokens[None], grad_weights

    return per_device


def solution(mesh):
    dp_count, seq_count = mesh.shape["dp"], mesh.shape["seq"]
    side = 4 if dp_count >= 16 else (2 if dp_count >= 4 else 1)
    specs = (P("dp", "seq", None), P("dp", "seq", None), P("seq", None, None))
    return jax.shard_map(
        make_device(side, side, dp_count, seq_count),
        mesh=mesh, in_specs=specs, out_specs=specs, check_vma=False)
```
